256 devices in a mesh: pipe: 4 (over x), expert: 16 (over y, z_hi), dp: 4 (over z_lo, core).
Axes of the slice: x: 4, y: 4, z: 8 (z_hi: 4, z_lo: 2; z = z_hi * 2 + z_lo), core: 2. Of those that a mesh axis runs over, the one named last changes fastest.
Arguments:
- tokens: bfloat16 [4, 2, 1024, 3584], P('pipe', None, 'expert'), may hold values from -6 to 6
- cotangent: bfloat16 [4, 2, 1024, 3584], P('pipe', None, 'expert'), may hold values from -6 to 6
- gain: float32 [4, 3584], P('pipe'), may hold values from 0.1 to 1.9
- router: bfloat16 [4, 3584, 16], P('pipe'), may hold values from -0.09375 to 0.09375
- w_gate: bfloat16 [4, 16, 3584, 1024], P('pipe', 'expert', None, 'dp'), may hold values from -0.09375 to 0.09375
- w_up: bfloat16 [4, 16, 3584, 1024], P('pipe', 'expert', None, 'dp'), may hold values from -0.09375 to 0.09375
- w_down: bfloat16 [4, 16, 1024, 3584], P('pipe', 'expert', 'dp'), may hold values from -0.1875 to 0.1875
- expert_ids: int32 [4, 2, 1024, 2], P('pipe', None, 'expert'), may hold values from 0 to 15, all different within a row; in each aligned block of 64 rows (0 to 63, 64 to 127, ..., all dimensions but the last counted through in order) at most 8 rows name the same one
Outputs:
- section_out: bfloat16 [4, 2, 1024, 3584], P('pipe', None, 'expert')
- section_grad: bfloat16 [4, 2, 1024, 3584], P('pipe', None, 'expert')
The draws below stay inside these ranges and needn't reach their ends.
Inputs may be any that keep to these rules, and one draw needn't show every extreme that they name: `expert_ids`: in each aligned block of 64 rows (one index of expert, one layer, one micro-batch), every expert is named by exactly 8 rows.
All inputs are finite; a program needn't handle non-finite values.
Results may differ from the reference program's by a relative error of at most 0.015.
Values may be sent and summed in bfloat16 or wider, within the bound.
A program may use at most 128 MiB of HBM per device.

```python
import math
import jax
import jax.numpy as jnp
import numpy as np
from jax import lax

D = 3584
H = 1024
TOPK = 2
MB = 2
TOK_DEV = 64
EXPERTS = 16
TOKENS = 1024
CAP = 8
SECTIONS = 4
N_PIPE = 4
N_EXPERT = 16
N_DP = 4


def steps_of(stream_key, shape, cuts, low, largest):
    level = 1.0
    for dim, blocks in cuts:
        heights = jax.random.uniform(jax.random.fold_in(jax.random.fold_in(stream_key, 6), dim), (blocks,), jnp.float32, low / len(cuts), largest / len(cuts))
        level = level * jnp.repeat(jnp.exp(heights), shape[dim] // blocks).reshape((-1,) + (1,) * (len(shape) - 1 - dim))
    return level


def shared_out(stream_key, own, number, rows, amount, top, limit, lean):
    order = jax.random.permutation(stream_key, amount)
    heavy_load, common = load_shares(amount, rows * top, limit, lean, True), load_shares(amount, rows * top, limit, lean, False)
    places = jnp.arange(amount)

    def named(tallies, offset_by):
        used = int((tallies > 0).sum())
        fixed = max(1, used // 4)
        shifted = fixed + (places - fixed + offset_by * (used - fixed)) % max(1, amount - fixed)
        return jnp.zeros((amount,), jnp.int32).at[order[jnp.where(places < fixed, places, shifted)]].set(jnp.asarray(tallies, jnp.int32))

    tallies = jnp.where(number % 4 == 0, named(heavy_load, number // 4), named(common, number - number // 4 - 1))
    mixed = jax.random.permutation(jax.random.fold_in(own, 3), amount)
    giver, receiver = mixed[0:amount // 2 * 2:2], mixed[1:amount // 2 * 2:2]
    margin = jnp.minimum(tallies[giver] - 1, limit - tallies[receiver]) // 2
    margin = jnp.where((giver == order[0]) | (receiver == order[0]) | (tallies[receiver] == 0), 0, jnp.maximum(margin, 0))
    shifted = jax.random.randint(jax.random.fold_in(own, 4), (amount // 2,), 0, 1 << 20) % (margin + 1)
    tallies = tallies.at[giver].add(-shifted).at[receiver].add(shifted)
    labels = jnp.searchsorted(jnp.cumsum(tallies), jnp.arange(rows * top), side="right").astype(jnp.int32)
    grid = labels.reshape(top, rows).T
    grid = grid[jax.random.permutation(jax.random.fold_in(own, 1), rows)]
    offset_by = jax.random.randint(jax.random.fold_in(own, 2), (rows, 1), 0, top)
    return jnp.take_along_axis(grid, (jnp.arange(top)[None, :] + offset_by) % top, axis=1)


def load_shares(count, total, limit, lean, full):
    weights = [(1 << 20) // math.isqrt(rank ** lean) + 1 for rank in range(1, count + 1)]
    largest = limit if full else min(limit, max(-(-total // count), total * weights[0] // sum(weights)))
    least = 1 if total - largest >= count - 1 else 0
    given, spare = [largest] + [least] * (count - 1), total - largest - least * (count - 1)
    while spare > 0:
        candidates = [i for i in range(1, count) if given[i] < largest] or [i for i in range(1, count) if given[i] < limit]
        pool, left = sum([weights[i] for i in candidates]), spare
        for i in candidates:
            addition = min(limit - given[i], max(1, left * weights[i] // pool), spare)
            given[i] = given[i] + addition
            spare = spare - addition
    return np.array(given)


def gaussian(own_key, extent, width, reach, split=(), kind=jnp.bfloat16):
    drawn = width * jax.random.normal(own_key, extent, jnp.float32)
    if split:
        drawn = drawn * steps_of(own_key, extent, split, -0.22, 0.18)
    return jnp.clip(drawn, -reach, reach).astype(kind)


def setup_inputs(seed: int = 0) -> dict:
    keys = jax.random.split(jax.random.key(seed), 9)
    tokens = gaussian(keys[0], (SECTIONS, MB, TOKENS, D), 1.0, 6.0, ((0, 4), (2, 16)))
    cotangent = gaussian(keys[1], (SECTIONS, MB, TOKENS, D), 1.0, 6.0, ((0, 4), (2, 16)))
    gain = jnp.clip(1.0 + 0.18 * jax.random.normal(keys[2], (SECTIONS, D), jnp.float32), 0.1, 1.9)
    router = gaussian(keys[3], (SECTIONS, D, EXPERTS), D ** -0.5, 0.09375, ((0, 4),))
    w_gate = gaussian(keys[4], (SECTIONS, EXPERTS, D, H), D ** -0.5, 0.09375, ((0, 4), (1, 16), (3, 4)))
    w_up = gaussian(keys[5], (SECTIONS, EXPERTS, D, H), D ** -0.5, 0.09375, ((0, 4), (1, 16), (3, 4)))
    w_down = gaussian(keys[6], (SECTIONS, EXPERTS, H, D), H ** -0.5, 0.1875, ((0, 4), (1, 16), (2, 4)))
    expert_ids_keys = jax.random.split(jax.random.fold_in(keys[7], 1), SECTIONS * MB * TOKENS // TOK_DEV)
    expert_ids_turns = jax.random.permutation(jax.random.fold_in(keys[7], 3), SECTIONS * MB * TOKENS // TOK_DEV)
    expert_ids = jax.vmap(lambda own, number: shared_out(jax.random.fold_in(keys[7], 2), own, number, TOK_DEV, EXPERTS, TOPK, CAP, 0))(expert_ids_keys, expert_ids_turns).reshape((SECTIONS, MB, TOKENS, TOPK))
    return dict(tokens=tokens, cotangent=cotangent, gain=gain, router=router, w_gate=w_gate, w_up=w_up, w_down=w_down, expert_ids=expert_ids)


route_scale = 2.5
norm_eps = 1e-06

def front(hidden, layer_gain, layer_router, routes):
    hidden_f = hidden.astype(jnp.float32)
    inverse = lax.rsqrt(lax.optimization_barrier(jnp.mean(hidden_f * hidden_f, axis=-1, keepdims=True)) + norm_eps)
    normed = (hidden_f * inverse * layer_gain).astype(jnp.bfloat16)
    logits = jnp.dot(normed, layer_router, preferred_element_type=jnp.float32)
    matches = routes[:, :, None] == jnp.arange(layer_router.shape[1], dtype=jnp.int32)[None, None, :]
    picked = lax.optimization_barrier(jnp.sum(jnp.where(matches, logits[:, None, :], 0.0), axis=-1))
    chosen = jax.nn.sigmoid(picked)
    weights = route_scale * chosen / lax.optimization_barrier(jnp.sum(chosen, axis=-1, keepdims=True))
    return (normed, inverse, chosen, weights)

def places(block_routes):
    flat = block_routes.reshape(-1)
    matches = (flat[:, None] == jnp.arange(N_EXPERT, dtype=jnp.int32)[None, :]).astype(jnp.int32)
    ranks = jnp.cumsum(matches, axis=0) - matches
    return (lax.optimization_barrier(jnp.sum(ranks * matches, axis=1)) * N_EXPERT + flat).astype(jnp.int32)

def fill_block(rows, target):
    empty = jnp.zeros((CAP * N_EXPERT, D), jnp.bfloat16)
    return empty.at[target].set(rows)

def read_block(buffer, target):
    return buffer[target]

def to_experts(values, target):
    blocks = values.reshape(N_EXPERT, TOK_DEV * TOPK, D)
    buffers = jax.vmap(fill_block)(blocks, target).reshape(N_EXPERT, CAP, N_EXPERT, D)
    return jnp.transpose(buffers, (2, 0, 1, 3)).reshape(N_EXPERT, N_EXPERT * CAP, D)

def from_experts(rows, target):
    buffers = rows.reshape(N_EXPERT, N_EXPERT, CAP, D)
    buffers = jnp.transpose(buffers, (1, 2, 0, 3)).reshape(N_EXPERT, CAP * N_EXPERT, D)
    return jax.vmap(read_block)(buffers, target).reshape(TOKENS, TOPK, D)

def expert_forward(pack):
    rows, gate_w, up_w, down_w = (pack[0], pack[1], pack[2], pack[3])
    gate_val = jnp.dot(rows, gate_w, preferred_element_type=jnp.float32)
    up_val = jnp.dot(rows, up_w, preferred_element_type=jnp.float32)
    activated = lax.optimization_barrier((jax.nn.silu(gate_val) * up_val).astype(jnp.bfloat16)).astype(jnp.float32)
    blocks = activated.reshape(rows.shape[0], N_DP, H // N_DP)
    down_blocks = down_w.astype(jnp.float32).reshape(N_DP, H // N_DP, D)
    partial_value = jnp.einsum('rph,phd->prd', blocks, down_blocks, precision=lax.Precision.HIGHEST)
    rounded = lax.optimization_barrier(partial_value.astype(jnp.bfloat16)).astype(jnp.float32)
    return lax.optimization_barrier(jnp.sum(rounded, axis=0)).astype(jnp.bfloat16)

def expert_backward(pack):
    rows, grads, gate_w, up_w, down_w = (pack[0], pack[1], pack[2], pack[3], pack[4])
    gate_val = jnp.dot(rows, gate_w, preferred_element_type=jnp.float32)
    up_val = jnp.dot(rows, up_w, preferred_element_type=jnp.float32)
    act_grad = jnp.dot(grads, down_w.T, preferred_element_type=jnp.float32)
    sigma = jax.nn.sigmoid(gate_val)
    gate_grad = (act_grad * up_val * sigma * (1.0 + gate_val * (1.0 - sigma))).astype(jnp.bfloat16)
    up_grad = (act_grad * gate_val * sigma).astype(jnp.bfloat16)
    gate_blocks = lax.optimization_barrier(gate_grad).astype(jnp.float32).reshape(rows.shape[0], N_DP, H // N_DP)
    up_blocks = lax.optimization_barrier(up_grad).astype(jnp.float32).reshape(rows.shape[0], N_DP, H // N_DP)
    gate_w_blocks = gate_w.astype(jnp.float32).reshape(D, N_DP, H // N_DP)
    up_w_blocks = up_w.astype(jnp.float32).reshape(D, N_DP, H // N_DP)
    partial_value = jnp.einsum('rph,dph->prd', gate_blocks, gate_w_blocks, precision=lax.Precision.HIGHEST)
    partial_value = partial_value + jnp.einsum('rph,dph->prd', up_blocks, up_w_blocks, precision=lax.Precision.HIGHEST)
    rounded = lax.optimization_barrier(partial_value.astype(jnp.bfloat16)).astype(jnp.float32)
    return lax.optimization_barrier(jnp.sum(rounded, axis=0)).astype(jnp.bfloat16)

def input_gradient(hidden, grad_f, layer_gain, layer_router, routes, inverse, chosen, weights, weight_grad, input_grad):
    total = lax.optimization_barrier(jnp.sum(weight_grad * weights, axis=-1, keepdims=True))
    chosen_grad = (route_scale * weight_grad - total) / lax.optimization_barrier(jnp.sum(chosen, axis=-1, keepdims=True))
    pick_grad = chosen_grad * chosen * (1.0 - chosen)
    matches = routes[:, :, None] == jnp.arange(layer_router.shape[1], dtype=jnp.int32)[None, None, :]
    logit_grad = lax.optimization_barrier(jnp.sum(jnp.where(matches, pick_grad[:, :, None], 0.0), axis=1))
    normed_grad = lax.optimization_barrier(jnp.sum(input_grad.astype(jnp.float32), axis=1))
    normed_grad = normed_grad + jnp.dot(logit_grad, layer_router.astype(jnp.float32).T, precision=lax.Precision.HIGHEST)
    hidden_f = hidden.astype(jnp.float32)
    scaled = layer_gain * normed_grad
    correction = lax.optimization_barrier(jnp.mean(hidden_f * scaled, axis=-1, keepdims=True))
    return (grad_f + inverse * scaled - hidden_f * inverse * inverse * inverse * correction).astype(jnp.bfloat16)

def reference(tokens, cotangent, gain, router, w_gate, w_up, w_down, expert_ids):
    out_rows = []
    grad_rows = []
    for section in range(N_PIPE):
        section_outs = []
        section_grads = []
        for micro in range(MB):
            hidden = tokens[section, micro]
            routes = expert_ids[section, micro]
            normed, inverse, chosen, weights = front(hidden, gain[section], router[section], routes)
            target = jax.vmap(places)(routes.reshape(N_EXPERT, TOK_DEV, TOPK))
            spread = jnp.broadcast_to(normed[:, None, :], (TOKENS, TOPK, D))
            rows = to_experts(spread, target)
            outputs = lax.map(expert_forward, (rows, w_gate[section], w_up[section], w_down[section]))
            expert_out = from_experts(outputs, target)
            result = hidden.astype(jnp.float32) + lax.optimization_barrier(jnp.sum(weights[:, :, None] * expert_out.astype(jnp.float32), axis=1))
            section_outs.append(result.astype(jnp.bfloat16))
            grad_f = cotangent[section, micro].astype(jnp.float32)
            out_grad = (weights[:, :, None] * grad_f[:, None, :]).astype(jnp.bfloat16)
            weight_grad = lax.optimization_barrier(jnp.sum(grad_f[:, None, :] * expert_out.astype(jnp.float32), axis=-1))
            grad_buffers = to_experts(out_grad, target)
            back = lax.map(expert_backward, (rows, grad_buffers, w_gate[section], w_up[section], w_down[section]))
            input_grad = from_experts(back, target)
            section_grads.append(input_gradient(hidden, grad_f, gain[section], router[section], routes, inverse, chosen, weights, weight_grad, input_grad))
        out_rows.append(jnp.stack(section_outs))
        grad_rows.append(jnp.stack(section_grads))
    layer_out = jnp.stack(out_rows)
    layer_grad = jnp.stack(grad_rows)
    return (jnp.roll(layer_out, 1, axis=0), jnp.roll(layer_grad, -1, axis=0))
```

```python
import jax
import jax.numpy as jnp
from jax import lax
from jax.experimental import pallas as pl
from jax.experimental.pallas import tpu as pltpu
from jax.sharding import PartitionSpec as P

MESH = pl.DeviceIdType.MESH
F32 = jnp.float32
BF16 = jnp.bfloat16
HIGHEST = lax.Precision.HIGHEST

route_scale = 2.5
norm_eps = 1e-06

D = 3584
HID = 256
TOK = 128
ROWS = 256
HALF = D // 2
QUART = D // 4
CH = 256
KCH = 896


def loop(count, body):
    def step(i, carry):
        body(i)
        return carry

    lax.fori_loop(0, count, step, 0)


def dot(a, b):
    return jnp.dot(a, b, preferred_element_type=F32)


def dot_nt(a, b, precision=None):
    return lax.dot_general(
        a, b, (((1,), (1,)), ((), ())), preferred_element_type=F32, precision=precision
    )


def iota(shape, dim):
    return lax.broadcasted_iota(jnp.int32, shape, dim)


def at128(start, size):
    return pl.ds(pl.multiple_of(start, 128), size)


def at16(start, size):
    return pl.ds(pl.multiple_of(start, 16), size)


def split(value):
    high = value.astype(BF16)
    return high, (value - high.astype(F32)).astype(BF16)


def kernel(
    tok_h,
    cot_h,
    gain,
    rout_h,
    wg_h,
    wu_h,
    wd_h,
    ids,
    out_h,
    grad_h,
    hid,
    cot,
    rout,
    wg,
    wu,
    wd,
    sel,
    com,
    cwh,
    cwl,
    inv_s,
    log_s,
    send,
    full,
    act_g,
    gv,
    uv,
    act,
    gg,
    ug,
    sc,
    scs,
    scr,
    es,
    eo,
    er,
    cp,
    pa,
    pb,
    pc,
    fa,
    fb,
    fc,
    ret,
    fin,
    res,
    lsem,
    d_s,
    d_r,
    f_s,
    f_r,
    s_s,
    s_r,
    e_s,
    e_r,
    p_s,
    p_r,
    r_s,
    r_r,
    a_s,
    a_r,
    c_s,
    c_r,
    x_s,
    x_r,
    o_s,
    o_r,
    q_s,
    q_r,
):
    px = lax.axis_index("pipe")
    ex = lax.axis_index("expert")
    dx = lax.axis_index("dp")
    y = ex // 4
    zh = ex % 4
    zl = dx // 2
    c = dx % 2
    near = (zh + 2 * zl + 3) % 4
    far = (zh + 2) % 4
    opp = (zh + 5 - 2 * zl) % 4
    me = zh * 4 + y
    other = 1 - zl
    ys = [(y + dy) % 4 for dy in range(4)]
    yb = [(y + 4 - dy) % 4 for dy in range(4)]

    def dev(zh_, y_, zl_, c_):
        return (px, y_ * 4 + zh_, zl_ * 2 + c_)

    sibling = dev(zh, y, zl, 1 - c)
    partner = dev(zh, y, other, c)
    diagonal = dev(zh, y, other, 1 - c)
    after = ((px + 1) % 4, ex, dx)
    before = ((px + 3) % 4, ex, dx)

    def remote(src, dst, ssem, rsem, device):
        return pltpu.make_async_remote_copy(
            src_ref=src,
            dst_ref=dst,
            send_sem=ssem,
            recv_sem=rsem,
            device_id=device,
            device_id_type=MESH,
        )

    barrier = pltpu.get_barrier_semaphore()
    greet = [sibling, partner, diagonal, after, before]
    for dy in range(4):
        greet += [
            dev(near, ys[dy], other, c),
            dev(far, ys[dy], other, c),
            dev(near, ys[dy], zl, c),
            dev(opp, ys[dy], zl, c),
        ]
        if dy:
            greet.append(dev(zh, ys[dy], zl, c))
    for device in greet:
        pl.semaphore_signal(barrier, inc=1, device_id=device, device_id_type=MESH)

    loads = [
        pltpu.make_async_copy(a, b, lsem.at[i])
        for i, (a, b) in enumerate(
            [(cot_h, cot), (tok_h, hid), (wd_h, wd), (rout_h, rout), (wg_h, wg), (wu_h, wu)]
        )
    ]
    for load in loads:
        load.start()

    slot = iota((TOK, ROWS), 1)
    token = iota((TOK, ROWS), 0)
    slot_e = (slot // 16 % 4) * 4 + slot // 64
    first, second = ids[:, 0:1], ids[:, 1:2]
    named = ((first == slot_e) | (second == slot_e)) & (token // 64 == slot // 8 % 2)
    named = jnp.where(named, 1.0, 0.0)
    earlier = jnp.where(iota((TOK, TOK), 1) < iota((TOK, TOK), 0), 1.0, 0.0).astype(BF16)
    rank = dot(earlier, named.astype(BF16))
    picks = jnp.where(rank == (slot % 8).astype(F32), named, 0.0)
    com[...] = picks
    sel[...] = picks.T.astype(BF16)

    half = c * HALF
    loads[0].wait()

    def gather_cot(i):
        cols = at128(half + i * CH, CH)
        send[0, :, at128(i * CH, CH)] = dot(sel[...], cot[:, cols]).astype(BF16)

    loop(HALF // CH, gather_cot)
    pl.semaphore_wait(barrier, len(greet))

    mine = at16(me * 16, 16)

    def dispatch(k):
        copies = []
        for dy in range(4):
            rows = at16((near * 4 + ys[dy]) * 16, 16)
            copies.append(
                remote(
                    send.at[k, rows, :],
                    full.at[k, mine, at128(half, HALF)],
                    d_s.at[k, dy],
                    d_r.at[k, dy],
                    dev(near, ys[dy], other, c),
                )
            )
        for dy in range(4):
            rows = at16((far * 4 + ys[dy]) * 16, 16)
            copies.append(
                remote(
                    send.at[k, rows, at128(zl * QUART, QUART)],
                    full.at[k, mine, at128(half + zl * QUART, QUART)],
                    d_s.at[k, 4 + dy],
                    d_r.at[k, 4 + dy],
                    dev(far, ys[dy], other, c),
                )
            )
        for dy in range(1, 4):
            rows = at16((zh * 4 + ys[dy]) * 16, 16)
            copies.append(
                remote(
                    send.at[k, rows, :],
                    full.at[k, mine, at128(half, HALF)],
                    d_s.at[k, 7 + dy],
                    d_r.at[k, 7 + dy],
                    dev(zh, ys[dy], zl, c),
                )
            )
        for copy in copies:
            copy.start()
        full[k, mine, at128(half, HALF)] = send[k, mine, :]
        return copies

    sent = []
    sent_u = dispatch(0)

    loads[1].wait()

    def squares(i, total):
        part = hid[:, at128(i * CH, CH)].astype(F32)
        return total + part * part

    total = lax.fori_loop(0, D // CH, squares, jnp.zeros((TOK, CH), F32))
    inv = lax.rsqrt(jnp.sum(total, axis=1, keepdims=True) / D + norm_eps)
    inv_s[...] = inv

    def normed(cols):
        return (hid[:, cols].astype(F32) * inv_s[...] * gain[:, cols]).astype(BF16)

    def gather_hid(i):
        cols = at128(half + i * CH, CH)
        send[1, :, at128(i * CH, CH)] = dot(sel[...], normed(cols)).astype(BF16)

    loop(HALF // CH, gather_hid)
    sent_x = dispatch(1)

    loads[3].wait()

    def route(i, total):
        cols = at128(i * CH, CH)
        return total + dot(normed(cols), rout[cols, :])

    logits = lax.fori_loop(0, D // CH, route, jnp.zeros((TOK, 16), F32))
    log_s[...] = logits

    def chosen_parts():
        lane = iota((TOK, 16), 1)
        mask = jnp.where((ids[:, 0:1] == lane) | (ids[:, 1:2] == lane), 1.0, 0.0)
        sig = jax.nn.sigmoid(log_s[...])
        csum = jnp.sum(mask * sig, axis=1, keepdims=True)
        return mask, sig, csum, route_scale * sig * mask / csum

    spread = iota((16, ROWS), 1)
    spread = jnp.where((spread // 16 % 4) * 4 + spread // 64 == iota((16, ROWS), 0), 1.0, 0.0)
    mask, sig, csum, w16 = chosen_parts()
    w_high, w_low = split(w16)
    cwh[...] = (dot(w_high, spread.astype(BF16)) * com[...]).astype(BF16)
    cwl[...] = (dot(w_low, spread.astype(BF16)) * com[...]).astype(BF16)

    def forward(k, sent_k):
        copies = []
        for dy in range(4):
            sent_k[dy].wait_recv()
            block = full.at[k, at16((near * 4 + yb[dy]) * 16, 16), at128(half, HALF)]
            copies.append(remote(block, block, f_s.at[k, dy], f_r.at[k, dy], partner))
            copies[-1].start()
        for dy in range(4):
            sent_k[4 + dy].wait_recv()
            block = full.at[
                k,
                at16((far * 4 + yb[dy]) * 16, 16),
                at128(half + other * QUART, QUART),
            ]
            copies.append(remote(block, block, f_s.at[k, 4 + dy], f_r.at[k, 4 + dy], partner))
            copies[-1].start()
        return copies

    def to_sibling(k, place, zh_):
        block = full.at[k, at16(zh_ * 64, 64), at128(half, HALF)]
        copy = remote(block, block, s_s.at[k, place], s_r.at[k, place], sibling)
        copy.start()
        return copy

    def share_early(k, sent_k):
        for dy in range(1, 4):
            sent_k[7 + dy].wait_recv()
        return [to_sibling(k, 0, near), to_sibling(k, 1, zh)]

    def share_late(k, fwd):
        for dy in range(4):
            fwd[dy].wait_recv()
        first = to_sibling(k, 2, opp)
        for dy in range(4):
            fwd[4 + dy].wait_recv()
        return [first, to_sibling(k, 3, far)]

    fwd_u = forward(0, sent_u)
    sib = share_early(0, sent_u)
    fwd_x = forward(1, sent_x)
    sib += share_late(0, fwd_u)
    sib_x = share_early(1, sent_x)
    for copy in sib:
        copy.wait_recv()
    loads[2].wait()

    def act_grad(i, total):
        cols = at128(i * KCH, KCH)
        return total + dot_nt(full[0, :, cols], wd[:, cols])

    act_g[...] = lax.fori_loop(0, D // KCH, act_grad, jnp.zeros((ROWS, HID), F32))
    sib_x += share_late(1, fwd_x)
    loads[4].wait()
    loads[5].wait()
    for copy in sib_x:
        copy.wait_recv()
    sib += sib_x

    def expand(weight):
        def step(i, total):
            cols = at128(i * KCH, KCH)
            return total + dot(full[1, :, cols], weight[cols, :])

        return lax.fori_loop(0, D // KCH, step, jnp.zeros((ROWS, HID), F32))

    gv[...] = expand(wg)
    uv[...] = expand(wu)
    g, u, a = gv[...], uv[...], act_g[...]
    sigma = jax.nn.sigmoid(g)
    act[...] = (g * sigma * u).astype(BF16)
    gg[...] = (a * u * sigma * (1.0 + g * (1.0 - sigma))).astype(BF16)
    ug[...] = (a * g * sigma).astype(BF16)

    def down(cols):
        return dot(act[...], wd[:, cols])

    def back(cols):
        return dot_nt(gg[...], wg[cols, :]) + dot_nt(ug[...], wu[cols, :])

    theirs = (1 - c) * HALF
    swaps = []
    for k, term in ((0, down), (1, back)):

        def for_sibling(i, k=k, term=term):
            es[k, :, at128(i * CH, CH)] = term(at128(theirs + i * CH, CH)).astype(BF16)

        loop(HALF // CH, for_sibling)
        swaps.append(remote(es.at[k], er.at[k], e_s.at[k], e_r.at[k], sibling))
        swaps[-1].start()

        def for_self(i, k=k, term=term):
            eo[k, :, at128(i * CH, CH)] = term(at128(half + i * CH, CH))

        if k == 0:
            loop(HALF // CH, for_self)
            ones = jnp.ones((8, HID), F32)
            w_row = dot_nt(ones, act[...].astype(F32) * act_g[...], HIGHEST)
            n_row = dot_nt(
                ones,
                gg[...].astype(F32) * gv[...] + ug[...].astype(F32) * uv[...],
                HIGHEST,
            )
            line = iota((8, ROWS), 0)
            sc[dx] = jnp.where(line == 0, w_row, jnp.where(line == 1, n_row, 0.0))
            marks = [
                remote(sc.at[dx], sc.at[dx], a_s.at[i], a_r.at[i], device)
                for i, device in enumerate((sibling, partner, diagonal))
            ]
            for copy in marks:
                copy.start()
        else:
            last_self = for_self

    def chip_sum(k):
        swaps[k].wait_recv()

        def add(i):
            cols = at128(i * CH, CH)
            cp[k, :, cols] = (eo[k, :, cols] + er[k, :, cols].astype(F32)).astype(BF16)

        loop(HALF // CH, add)
        copies = [
            remote(cp.at[k, at16(opp * 64, 64), :], pa.at[k], p_s.at[k, 0], p_r.at[k, 0], partner),
            remote(
                cp.at[k, at16(far * 64, 64), at128(zl * QUART, QUART)],
                pb.at[k],
                p_s.at[k, 1],
                p_r.at[k, 1],
                partner,
            ),
            remote(
                cp.at[k, at16(zh * 64, 64), at128(other * QUART, QUART)],
                pc.at[k],
                p_s.at[k, 2],
                p_r.at[k, 2],
                partner,
            ),
        ]
        for copy in copies:
            copy.start()
        return copies

    pairs = [chip_sum(0)]
    loop(HALF // CH, last_self)
    pairs.append(chip_sum(1))

    for copy in marks:
        copy.wait_recv()
    scs[...] = (sc[0] + sc[1]) + (sc[2] + sc[3])
    routes_back = []
    for dy in range(4):
        routes_back += [
            (near, dy, other, 0),
            (near, dy, zl, 1),
            (far, dy, other, 2),
        ]
        if dy:
            routes_back.append((zh, dy, zl, 3))
    notes = []
    for i, (zh_, dy, zl_, kind) in enumerate(routes_back):
        notes.append(
            remote(
                scs.at[:, at128((zh_ // 2) * 128, 128)],
                scr.at[pl.ds(pl.multiple_of(me * 8, 8), 8), :],
                c_s.at[i],
                c_r.at[i],
                dev(zh_, ys[dy], zl_, c),
            )
        )
        notes[-1].start()
    scr[pl.ds(pl.multiple_of(me * 8, 8), 8), :] = scs[:, at128((zh // 2) * 128, 128)]

    def give_back(k):
        pairs[k][0].wait_recv()
        fa[k] = (cp[k, at16(near * 64, 64), :].astype(F32) + pa[k].astype(F32)).astype(BF16)
        pairs[k][1].wait_recv()
        fb[k] = (
            cp[k, at16(far * 64, 64), at128(other * QUART, QUART)].astype(F32)
            + pb[k].astype(F32)
        ).astype(BF16)
        pairs[k][2].wait_recv()
        fc[k] = (
            cp[k, at16(zh * 64, 64), at128(zl * QUART, QUART)].astype(F32) + pc[k].astype(F32)
        ).astype(BF16)
        copies = []
        for i, (zh_, dy, zl_, kind) in enumerate(routes_back):
            rows = at16(ys[dy] * 16, 16)
            if kind == 0:
                src = fa.at[k, rows, at128(other * QUART, QUART)]
            elif kind == 1:
                src = fa.at[k, rows, at128(zl * QUART, QUART)]
            elif kind == 2:
                src = fb.at[k, rows, :]
            else:
                src = fc.at[k, rows, :]
            copies.append(
                remote(
                    src,
                    ret.at[k, mine, :],
                    r_s.at[k, i],
                    r_r.at[k, i],
                    dev(zh_, ys[dy], zl_, c),
                )
            )
            copies[-1].start()
        ret[k, mine, :] = fc[k, at16(y * 16, 16), :]
        return copies

    backs = [give_back(0), give_back(1)]

    quarter = at128(half + zl * QUART, QUART)

    def combine(k):
        for copy in backs[k]:
            copy.wait_recv()
        return dot(cwh[...], ret[k]) + dot(cwl[...], ret[k])

    shifts = []

    def ship(k, device):
        shifts.append(
            remote(fin.at[k], res.at[k, :, quarter], x_s.at[k], x_r.at[k], device)
        )
        shifts[-1].start()

    fin[0] = (hid[:, quarter].astype(F32) + combine(0)).astype(BF16)
    ship(0, after)

    for copy in notes:
        copy.wait_recv()
    lane_at = (me % 8) * 16
    turn = jnp.where(iota((128, ROWS), 0) == lane_at + iota((128, ROWS), 1) % 16, 1.0, 0.0)
    moved = jnp.dot(scr[...], turn, precision=HIGHEST, preferred_element_type=F32)
    row, col = iota((128, ROWS), 0), iota((128, ROWS), 1)
    own_row = row // 8 == col // 16
    w_row = jnp.sum(jnp.where(own_row & (row % 8 == 0), moved, 0.0), axis=0, keepdims=True)
    n_row = jnp.sum(jnp.where(own_row & (row % 8 == 1), moved, 0.0), axis=0, keepdims=True)
    mask, sig, csum, w16 = chosen_parts()
    weight_grad = dot_nt(com[...] * w_row, spread, HIGHEST)
    total = jnp.sum(weight_grad * w16, axis=1, keepdims=True)
    logit_grad = (route_scale * weight_grad - total) / csum * sig * (1.0 - sig) * mask
    weighted = cwh[...].astype(F32) + cwl[...].astype(F32)
    inner = jnp.sum(weighted * n_row, axis=1, keepdims=True) + jnp.sum(
        logit_grad * log_s[...], axis=1, keepdims=True
    )
    l_high, l_low = split(logit_grad)
    inverse = inv_s[...]
    pull = inverse * inverse * inner / D

    routers = rout[quarter, :]
    normed_grad = combine(1) + (dot_nt(l_high, routers) + dot_nt(l_low, routers))
    fin[1] = (
        cot[:, quarter].astype(F32)
        + inverse * gain[:, quarter] * normed_grad
        - hid[:, quarter].astype(F32) * pull
    ).astype(BF16)
    ship(1, before)

    spreads = []
    for k in range(2):
        shifts[k].wait_recv()
        block = res.at[k, :, quarter]
        spreads.append(remote(block, block, o_s.at[k], o_r.at[k], partner))
        spreads[-1].start()
    cores = []
    for k in range(2):
        spreads[k].wait_recv()
        block = res.at[k, :, at128(half, HALF)]
        cores.append(remote(block, block, q_s.at[k], q_r.at[k], sibling))
        cores[-1].start()
    stores = []
    for k, target in ((0, out_h), (1, grad_h)):
        cores[k].wait_recv()
        stores.append(pltpu.make_async_copy(res.at[k], target, lsem.at[6 + k]))
        stores[-1].start()

    for copy in (
        sent_u
        + sent_x
        + fwd_u
        + fwd_x
        + sib
        + swaps
        + marks
        + notes
        + pairs[0]
        + pairs[1]
        + backs[0]
        + backs[1]
        + shifts
        + spreads
        + cores
    ):
        copy.wait_send()
    for copy in stores:
        copy.wait()


def shards(tokens, cotangent, gain, router, w_gate, w_up, w_down, expert_ids):
    anywhere = pl.BlockSpec(memory_space=pl.ANY)
    vmem = pl.BlockSpec(memory_space=pltpu.VMEM)

    def buf(*shape, dtype=BF16):
        return pltpu.VMEM(shape, dtype)

    def sems(*shape):
        return pltpu.SemaphoreType.DMA(shape)

    scratch = [
        buf(TOK, D),
        buf(TOK, D),
        buf(D, 16),
        buf(D, HID),
        buf(D, HID),
        buf(HID, D),
        buf(ROWS, TOK),
        buf(TOK, ROWS, dtype=F32),
        buf(TOK, ROWS),
        buf(TOK, ROWS),
        buf(TOK, 1, dtype=F32),
        buf(TOK, 16, dtype=F32),
        buf(2, ROWS, HALF),
        buf(2, ROWS, D),
        buf(ROWS, HID, dtype=F32),
        buf(ROWS, HID, dtype=F32),
        buf(ROWS, HID, dtype=F32),
        buf(ROWS, HID),
        buf(ROWS, HID),
        buf(ROWS, HID),
        buf(4, 8, ROWS, dtype=F32),
        buf(8, ROWS, dtype=F32),
        buf(128, 128, dtype=F32),
        buf(2, ROWS, HALF),
        buf(2, ROWS, HALF, dtype=F32),
        buf(2, ROWS, HALF),
        buf(2, ROWS, HALF),
        buf(2, 64, HALF),
        buf(2, 64, QUART),
        buf(2, 64, QUART),
        buf(2, 64, HALF),
        buf(2, 64, QUART),
        buf(2, 64, QUART),
        buf(2, ROWS, QUART),
        buf(2, TOK, QUART),
        buf(2, TOK, D),
        sems(8),
        sems(2, 11),
        sems(2, 11),
        sems(2, 8),
        sems(2, 8),
        sems(2, 4),
        sems(2, 4),
        sems(2),
        sems(2),
        sems(2, 3),
        sems(2, 3),
        sems(2, 15),
        sems(2, 15),
        sems(3),
        sems(3),
        sems(15),
        sems(15),
        sems(2),
        sems(2),
        sems(2),
        sems(2),
        sems(2),
        sems(2),
    ]
    out = jax.ShapeDtypeStruct((TOK, D), BF16)
    section_out, section_grad = pl.pallas_call(
        kernel,
        out_shape=(out, out),
        in_specs=[anywhere, anywhere, vmem, anywhere, anywhere, anywhere, anywhere, vmem],
        out_specs=(anywhere, anywhere),
        scratch_shapes=scratch,
        compiler_params=pltpu.CompilerParams(
            collective_id=0, has_side_effects=True, vmem_limit_bytes=56 * 1024 * 1024
        ),
    )(
        tokens.reshape(TOK, D),
        cotangent.reshape(TOK, D),
        gain,
        router.reshape(D, 16),
        w_gate.reshape(D, HID),
        w_up.reshape(D, HID),
        w_down.reshape(HID, D),
        expert_ids.reshape(TOK, 2),
    )
    return section_out.reshape(tokens.shape), section_grad.reshape(tokens.shape)


def solution(mesh):
    in_specs = (
        P("pipe", None, "expert", None),
        P("pipe", None, "expert", None),
        P("pipe", None),
        P("pipe", None, None),
        P("pipe", "expert", None, "dp"),
        P("pipe", "expert", None, "dp"),
        P("pipe", "expert", "dp", None),
        P("pipe", None, "expert", None),
    )
    out_specs = (P("pipe", None, "expert", None), P("pipe", None, "expert", None))
    return jax.shard_map(shards, mesh=mesh, in_specs=in_specs, out_specs=out_specs, check_vma=False)
```

```python
import jax
import jax.numpy as jnp
from jax import lax
from jax.experimental import pallas as pl
from jax.experimental.pallas import tpu as pltpu
from jax.sharding import PartitionSpec as P

MESH = pl.DeviceIdType.MESH
F32 = jnp.float32
BF16 = jnp.bfloat16
HIGHEST = lax.Precision.HIGHEST

route_scale = 2.5
norm_eps = 1e-06

D = 3584
HID = 256
TOK = 128
ROWS = 256
HALF = D // 2
QUART = D // 4
PIECES = ((0, 0, 512), (0, 512, 384), (1, 0, 512), (1, 512, 384))
COUNT = len(PIECES)


def dot(a, b):
    return jnp.dot(a, b, preferred_element_type=F32)


def dot_nt(a, b, precision=None):
    return lax.dot_general(
        a, b, (((1,), (1,)), ((), ())), preferred_element_type=F32, precision=precision
    )


def iota(shape, dim):
    return lax.broadcasted_iota(jnp.int32, shape, dim)


def at128(start, size):
    return pl.ds(pl.multiple_of(start, 128), size)


def at16(start, size):
    return pl.ds(pl.multiple_of(start, 16), size)


def at8(start, size):
    return pl.ds(pl.multiple_of(start, 8), size)


def split(value):
    high = value.astype(BF16)
    return high, (value - high.astype(F32)).astype(BF16)


def kernel(
    tok_h,
    cot_h,
    gain,
    rout,
    wg_h,
    wu_h,
    wd_h,
    ids,
    out_v,
    grad_v,
    hid,
    cot,
    nrm,
    wg,
    wu,
    wd,
    sel,
    com,
    cwh,
    cwl,
    inv_s,
    log_s,
    send,
    full,
    act_g,
    gv,
    uv,
    act,
    gg,
    ug,
    sc,
    scs,
    scr,
    lsem,
    d_s,
    d_r,
    f_s,
    f_r,
    s_s,
    s_r,
    e_s,
    e_r,
    p_s,
    p_r,
    r_s,
    r_r,
    a_s,
    a_r,
    c_s,
    c_r,
    x_s,
    x_r,
    *piece_refs,
):
    bufs = [piece_refs[i * 12 : (i + 1) * 12] for i in range(COUNT)]

    px = lax.axis_index("pipe")
    ex = lax.axis_index("expert")
    dx = lax.axis_index("dp")
    y = ex // 4
    zh = ex % 4
    zl = dx // 2
    c = dx % 2
    near = (zh + 2 * zl + 3) % 4
    far = (zh + 2) % 4
    opp = (zh + 5 - 2 * zl) % 4
    me = zh * 4 + y
    other = 1 - zl
    ys = [(y + dy) % 4 for dy in range(4)]
    yb = [(y + 4 - dy) % 4 for dy in range(4)]

    def dev(zh_, y_, zl_, c_):
        return (px, y_ * 4 + zh_, zl_ * 2 + c_)

    sibling = dev(zh, y, zl, 1 - c)
    partner = dev(zh, y, other, c)
    diagonal = dev(zh, y, other, 1 - c)
    after = ((px + 1) % 4, ex, dx)
    before = ((px + 3) % 4, ex, dx)

    everything = []

    def remote(src, dst, ssem, rsem, device):
        copy = pltpu.make_async_remote_copy(
            src_ref=src,
            dst_ref=dst,
            send_sem=ssem,
            recv_sem=rsem,
            device_id=device,
            device_id_type=MESH,
        )
        copy.start()
        everything.append(copy)
        return copy

    barrier = pltpu.get_barrier_semaphore()
    greet = [sibling, partner, diagonal, after, before]
    for dy in range(4):
        greet += [
            dev(near, ys[dy], other, c),
            dev(far, ys[dy], other, c),
            dev(near, ys[dy], zl, c),
            dev(opp, ys[dy], zl, c),
        ]
        if dy:
            greet.append(dev(zh, ys[dy], zl, c))
    for device in greet:
        pl.semaphore_signal(barrier, inc=1, device_id=device, device_id_type=MESH)

    loads = [
        pltpu.make_async_copy(a, b, lsem.at[i])
        for i, (a, b) in enumerate(
            [(tok_h, hid), (cot_h, cot), (wg_h, wg), (wu_h, wu), (wd_h, wd)]
        )
    ]
    for load in loads:
        load.start()

    slot = iota((ROWS, TOK), 0)
    token = iota((ROWS, TOK), 1)
    slot_e = ((slot >> 4) & 3) * 4 + (slot >> 6)
    first = jnp.concatenate([ids[0, 0:1, :], ids[1, 0:1, :]], axis=1)
    second = jnp.concatenate([ids[0, 1:2, :], ids[1, 1:2, :]], axis=1)
    named = ((first == slot_e) | (second == slot_e)) & ((token >> 6) == ((slot >> 3) & 1))
    named = jnp.where(named, 1.0, 0.0)
    earlier = jnp.where(iota((TOK, TOK), 0) < iota((TOK, TOK), 1), 1.0, 0.0).astype(BF16)
    rank = dot(named.astype(BF16), earlier)
    picks = jnp.where(rank == (slot & 7).astype(F32), named, 0.0)
    sel[...] = picks.astype(BF16)

    half = c * HALF
    loads[0].wait()
    total = jnp.zeros((TOK, 1), F32)
    for i in range(4):
        part = hid[:, i * QUART : (i + 1) * QUART].astype(F32)
        total = total + jnp.sum(part * part, axis=1, keepdims=True)
    inv_s[...] = lax.rsqrt(total / D + norm_eps)

    def norm(start):
        for i in range(2):
            cols = at128(start + i * QUART, QUART)
            nrm[:, cols] = (hid[:, cols].astype(F32) * inv_s[...] * gain[:, cols]).astype(BF16)

    def gather(k, source):
        for i in range(2):
            send[k, :, i * QUART : (i + 1) * QUART] = dot(
                sel[...], source[:, at128(half + i * QUART, QUART)]
            ).astype(BF16)

    norm(half)
    gather(0, nrm)
    pl.semaphore_wait(barrier, len(greet))

    mine = at16(me * 16, 16)

    def dispatch(k):
        copies = []
        for dy in range(4):
            rows = at16((near * 4 + ys[dy]) * 16, 16)
            copies.append(
                remote(
                    send.at[k, rows, :],
                    full.at[k, mine, at128(half, HALF)],
                    d_s.at[k, dy],
                    d_r.at[k, dy],
                    dev(near, ys[dy], other, c),
                )
            )
        for dy in range(4):
            rows = at16((far * 4 + ys[dy]) * 16, 16)
            copies.append(
                remote(
                    send.at[k, rows, at128(zl * QUART, QUART)],
                    full.at[k, mine, at128(half + zl * QUART, QUART)],
                    d_s.at[k, 4 + dy],
                    d_r.at[k, 4 + dy],
                    dev(far, ys[dy], other, c),
                )
            )
        for dy in range(1, 4):
            rows = at16((zh * 4 + ys[dy]) * 16, 16)
            copies.append(
                remote(
                    send.at[k, rows, :],
                    full.at[k, mine, at128(half, HALF)],
                    d_s.at[k, 7 + dy],
                    d_r.at[k, 7 + dy],
                    dev(zh, ys[dy], zl, c),
                )
            )
        full[k, mine, at128(half, HALF)] = send[k, mine, :]
        return copies

    sent_x = dispatch(0)
    loads[1].wait()
    gather(1, cot)
    sent_u = dispatch(1)

    com[...] = picks.T
    norm((1 - c) * HALF)
    log_s[...] = dot_nt(nrm[...], rout[...])
    spread = iota((16, ROWS), 1)
    spread = jnp.where(
        ((spread >> 4) & 3) * 4 + (spread >> 6) == iota((16, ROWS), 0), 1.0, 0.0
    )

    def chosen_parts():
        mask = dot_nt(com[...].astype(BF16), spread.astype(BF16))
        sig = jax.nn.sigmoid(log_s[...])
        csum = jnp.sum(mask * sig, axis=1, keepdims=True)
        return mask, sig, csum, route_scale * sig * mask / csum

    mask, sig, csum, w16 = chosen_parts()
    w_high, w_low = split(w16)
    cwh[...] = (dot(w_high, spread.astype(BF16)) * com[...]).astype(BF16)
    cwl[...] = (dot(w_low, spread.astype(BF16)) * com[...]).astype(BF16)

    def forward_near(k, sent):
        copies = []
        for dy in range(4):
            sent[dy].wait_recv()
            block = full.at[k, at16((near * 4 + yb[dy]) * 16, 16), at128(half, HALF)]
            copies.append(remote(block, block, f_s.at[k, dy], f_r.at[k, dy], partner))
        return copies

    def forward_far(k, sent):
        copies = []
        for dy in range(4):
            sent[4 + dy].wait_recv()
            block = full.at[
                k,
                at16((far * 4 + yb[dy]) * 16, 16),
                at128(half + other * QUART, QUART),
            ]
            copies.append(remote(block, block, f_s.at[k, 4 + dy], f_r.at[k, 4 + dy], partner))
        return copies

    def to_sibling(k, place, zh_):
        block = full.at[k, at16(zh_ * 64, 64), at128(half, HALF)]
        return remote(block, block, s_s.at[k, place], s_r.at[k, place], sibling)

    def share_own(k, sent):
        for dy in range(1, 4):
            sent[7 + dy].wait_recv()
        return to_sibling(k, 1, zh)

    def share(k, place, zh_, copies):
        for copy in copies:
            copy.wait_recv()
        return to_sibling(k, place, zh_)

    fwd_x = forward_near(0, sent_x)
    sib_x = [to_sibling(0, 0, near)]
    fwd_x += forward_far(0, sent_x)
    sib_x.append(share_own(0, sent_x))
    sib_x.append(share(0, 2, opp, fwd_x[:4]))
    sib_x.append(share(0, 3, far, fwd_x[4:]))
    fwd_u = forward_near(1, sent_u)
    sib_u = [to_sibling(1, 0, near)]
    for load in loads[2:]:
        load.wait()
    for copy in sib_x:
        copy.wait_recv()

    gv[...] = dot(full[0], wg[...])
    uv[...] = dot(full[0], wu[...])
    g = gv[...]
    act[...] = (g * jax.nn.sigmoid(g) * uv[...]).astype(BF16)

    def down(cols):
        return dot(act[...], wd[:, cols])

    def back(cols):
        return dot_nt(gg[...], wg[cols, :]) + dot_nt(ug[...], wu[cols, :])

    terms = (down, back)
    theirs = (1 - c) * HALF

    def swap(p):
        k, off, w = PIECES[p]
        es, er = bufs[p][0], bufs[p][2]
        for i in range(2):
            es[:, i * w : (i + 1) * w] = terms[k](at128(theirs + i * QUART + off, w)).astype(BF16)
        return remote(es, er, e_s.at[p], e_r.at[p], sibling)

    def keep(p):
        k, off, w = PIECES[p]
        eo = bufs[p][1]
        for i in range(2):
            eo[:, i * w : (i + 1) * w] = terms[k](at128(half + i * QUART + off, w))

    def pair_sum(p, swapped):
        w = PIECES[p][2]
        es, eo, er, cp, pa, pb, pc = bufs[p][:7]
        swapped.wait_recv()

        def add(zh_):
            rows = at16(zh_ * 64, 64)
            cp[rows, :] = (eo[rows, :] + er[rows, :].astype(F32)).astype(BF16)
            return rows

        rows = add(far)
        copies = [
            remote(cp.at[rows, at128(zl * w, w)], pb, p_s.at[p, 0], p_r.at[p, 0], partner)
        ]
        rows = add(opp)
        copies.append(remote(cp.at[rows, :], pa, p_s.at[p, 1], p_r.at[p, 1], partner))
        rows = add(zh)
        copies.append(
            remote(cp.at[rows, at128(other * w, w)], pc, p_s.at[p, 2], p_r.at[p, 2], partner)
        )
        add(near)
        return copies

    def give_back(p, pair):
        w = PIECES[p][2]
        cp, pa, pb, pc, fa, fb, fc, ret = bufs[p][3:11]
        copies = []

        def give(src, zh_, dy, zl_):
            i = len(copies)
            copies.append(
                remote(src, ret.at[mine, :], r_s.at[p, i], r_r.at[p, i], dev(zh_, ys[dy], zl_, c))
            )

        pair[0].wait_recv()
        fb[...] = (
            cp[at16(far * 64, 64), at128(other * w, w)].astype(F32) + pb[...].astype(F32)
        ).astype(BF16)
        for dy in range(4):
            give(fb.at[at16(ys[dy] * 16, 16), :], far, dy, other)
        pair[1].wait_recv()
        fa[...] = (cp[at16(near * 64, 64), :].astype(F32) + pa[...].astype(F32)).astype(BF16)
        for dy in range(4):
            rows = at16(ys[dy] * 16, 16)
            give(fa.at[rows, at128(zl * w, w)], near, dy, zl)
            give(fa.at[rows, at128(other * w, w)], near, dy, other)
        pair[2].wait_recv()
        fc[...] = (
            cp[at16(zh * 64, 64), at128(zl * w, w)].astype(F32) + pc[...].astype(F32)
        ).astype(BF16)
        for dy in range(1, 4):
            give(fc.at[at16(ys[dy] * 16, 16), :], zh, dy, zl)
        ret[mine, :] = fc[at16(y * 16, 16), :]
        return copies

    swaps = [swap(0), swap(1)]
    keep(0)
    fwd_u += forward_far(1, sent_u)
    sib_u.append(share_own(1, sent_u))
    pairs = [pair_sum(0, swaps[0])]
    sib_u.append(share(1, 2, opp, fwd_u[:4]))
    keep(1)
    pairs.append(pair_sum(1, swaps[1]))
    sib_u.append(share(1, 3, far, fwd_u[4:]))
    for copy in sib_u:
        copy.wait_recv()

    act_g[...] = dot_nt(full[1], wd[...])
    g, u, a = gv[...], uv[...], act_g[...]
    sigma = jax.nn.sigmoid(g)
    gg[...] = (a * u * sigma * (1.0 + g * (1.0 - sigma))).astype(BF16)
    ug[...] = (a * g * sigma).astype(BF16)
    swaps += [swap(2), swap(3)]

    ones = jnp.ones((8, HID), F32)
    w_row = dot_nt(ones, act[...].astype(F32) * act_g[...], HIGHEST)
    n_row = dot_nt(
        ones, gg[...].astype(F32) * gv[...] + ug[...].astype(F32) * uv[...], HIGHEST
    )
    line = iota((8, ROWS), 0)
    sc[dx] = jnp.where(line == 0, w_row, jnp.where(line == 1, n_row, 0.0))
    marks = [
        remote(sc.at[dx], sc.at[dx], a_s.at[i], a_r.at[i], device)
        for i, device in enumerate((sibling, partner, diagonal))
    ]
    keep(2)
    backs = [give_back(0, pairs[0])]
    pairs.append(pair_sum(2, swaps[2]))
    keep(3)
    backs.append(give_back(1, pairs[1]))
    pairs.append(pair_sum(3, swaps[3]))

    for copy in marks:
        copy.wait_recv()
    scs[...] = (sc[0] + sc[1]) + (sc[2] + sc[3])
    own_notes = at8(me * 8, 8)
    notes = []
    for dy in range(4):
        for zh_, zl_ in ((near, other), (near, zl), (far, other)) + (((zh, zl),) if dy else ()):
            i = len(notes)
            notes.append(
                remote(
                    scs.at[:, at128((zh_ // 2) * 128, 128)],
                    scr.at[own_notes, :],
                    c_s.at[i],
                    c_r.at[i],
                    dev(zh_, ys[dy], zl_, c),
                )
            )
    scr[own_notes, :] = scs[:, at128((zh // 2) * 128, 128)]

    quarter = half + zl * QUART
    results = (out_v, grad_v)

    def combine(p):
        ret = bufs[p][10]
        for copy in backs[p]:
            copy.wait_recv()
        return dot(cwh[...], ret[...]) + dot(cwl[...], ret[...])

    def ship(p, value, device):
        k, off, w = PIECES[p]
        fin = bufs[p][11]
        fin[...] = value.astype(BF16)
        return remote(
            fin, results[k].at[:, at128(quarter + off, w)], x_s.at[p, 0], x_r.at[p, 0], device
        )

    def pass_on(p, shift):
        k, off, w = PIECES[p]
        shift.wait_recv()
        block = results[k].at[:, at128(quarter + off, w)]
        return [
            remote(block, block, x_s.at[p, 1], x_r.at[p, 1], partner),
            remote(block, block, x_s.at[p, 2], x_r.at[p, 2], sibling),
        ]

    def pass_last(p, passed):
        k, off, w = PIECES[p]
        passed[0].wait_recv()
        block = results[k].at[:, at128(half + other * QUART + off, w)]
        passed.append(remote(block, block, x_s.at[p, 3], x_r.at[p, 3], sibling))

    shifts = []
    for p in range(2):
        k, off, w = PIECES[p]
        shifts.append(
            ship(p, hid[:, at128(quarter + off, w)].astype(F32) + combine(p), after)
        )
    backs.append(give_back(2, pairs[2]))
    passed = [pass_on(0, shifts[0])]
    backs.append(give_back(3, pairs[3]))
    passed.append(pass_on(1, shifts[1]))

    for copy in notes:
        copy.wait_recv()
    lane_at = (me % 8) * 16
    row, col = iota((128, ROWS), 0), iota((128, ROWS), 1)
    turn = jnp.where(row == lane_at + (col & 15), 1.0, 0.0)
    moved = jnp.dot(scr[...], turn, precision=HIGHEST, preferred_element_type=F32)
    own_row = (row >> 3) == (col >> 4)
    w_row = jnp.sum(jnp.where(own_row & ((row & 7) == 0), moved, 0.0), axis=0, keepdims=True)
    n_row = jnp.sum(jnp.where(own_row & ((row & 7) == 1), moved, 0.0), axis=0, keepdims=True)
    mask, sig, csum, w16 = chosen_parts()
    weight_grad = dot_nt(com[...] * w_row, spread, HIGHEST)
    total = jnp.sum(weight_grad * w16, axis=1, keepdims=True)
    logit_grad = (route_scale * weight_grad - total) / csum * sig * (1.0 - sig) * mask
    weighted = cwh[...].astype(F32) + cwl[...].astype(F32)
    inner = jnp.sum(weighted * n_row, axis=1, keepdims=True) + jnp.sum(
        logit_grad * log_s[...], axis=1, keepdims=True
    )
    l_high, l_low = split(logit_grad)
    inverse = inv_s[...]
    pull = inverse * inverse * inner / D

    def gradient(p):
        k, off, w = PIECES[p]
        cols = at128(quarter + off, w)
        routers = rout[:, cols]
        normed_grad = combine(p) + (dot(l_high, routers) + dot(l_low, routers))
        return (
            cot[:, cols].astype(F32)
            + inverse * gain[:, cols] * normed_grad
            - hid[:, cols].astype(F32) * pull
        )

    shifts.append(ship(2, gradient(2), before))
    pass_last(0, passed[0])
    pass_last(1, passed[1])
    shifts.append(ship(3, gradient(3), before))
    passed.append(pass_on(2, shifts[2]))
    passed.append(pass_on(3, shifts[3]))
    pass_last(2, passed[2])
    pass_last(3, passed[3])
    for copies in passed:
        copies[1].wait_recv()
        copies[2].wait_recv()
    for copy in everything:
        copy.wait_send()


def shards(tokens, cotangent, gain, router, w_gate, w_up, w_down, expert_ids):
    anywhere = pl.BlockSpec(memory_space=pl.ANY)
    vmem = pl.BlockSpec(memory_space=pltpu.VMEM)

    def buf(*shape, dtype=BF16):
        return pltpu.VMEM(shape, dtype)

    def sems(*shape):
        return pltpu.SemaphoreType.DMA(shape)

    scratch = [
        buf(TOK, D),
        buf(TOK, D),
        buf(TOK, D),
        buf(D, HID),
        buf(D, HID),
        buf(HID, D),
        buf(ROWS, TOK),
        buf(TOK, ROWS, dtype=F32),
        buf(TOK, ROWS),
        buf(TOK, ROWS),
        buf(TOK, 1, dtype=F32),
        buf(TOK, 16, dtype=F32),
        buf(2, ROWS, HALF),
        buf(2, ROWS, D),
        buf(ROWS, HID, dtype=F32),
        buf(ROWS, HID, dtype=F32),
        buf(ROWS, HID, dtype=F32),
        buf(ROWS, HID),
        buf(ROWS, HID),
        buf(ROWS, HID),
        buf(4, 8, ROWS, dtype=F32),
        buf(8, ROWS, dtype=F32),
        buf(128, 128, dtype=F32),
        sems(5),
        sems(2, 11),
        sems(2, 11),
        sems(2, 8),
        sems(2, 8),
        sems(2, 4),
        sems(2, 4),
        sems(COUNT),
        sems(COUNT),
        sems(COUNT, 3),
        sems(COUNT, 3),
        sems(COUNT, 15),
        sems(COUNT, 15),
        sems(3),
        sems(3),
        sems(15),
        sems(15),
        sems(COUNT, 4),
        sems(COUNT, 4),
    ]
    for _, _, w in PIECES:
        scratch += [
            buf(ROWS, 2 * w),
            buf(ROWS, 2 * w, dtype=F32),
            buf(ROWS, 2 * w),
            buf(ROWS, 2 * w),
            buf(64, 2 * w),
            buf(64, w),
            buf(64, w),
            buf(64, 2 * w),
            buf(64, w),
            buf(64, w),
            buf(ROWS, w),
            buf(TOK, w),
        ]
    out = pltpu.VMEM((TOK, D), BF16)
    section_out, section_grad = pl.pallas_call(
        kernel,
        out_shape=(out, out),
        in_specs=[anywhere, anywhere, vmem, vmem, anywhere, anywhere, anywhere, vmem],
        out_specs=(vmem, vmem),
        scratch_shapes=scratch,
        compiler_params=pltpu.CompilerParams(
            collective_id=0, has_side_effects=True, vmem_limit_bytes=56 * 1024 * 1024
        ),
    )(
        tokens.reshape(TOK, D),
        cotangent.reshape(TOK, D),
        gain,
        jnp.swapaxes(router.reshape(D, 16), 0, 1),
        w_gate.reshape(D, HID),
        w_up.reshape(D, HID),
        w_down.reshape(HID, D),
        jnp.swapaxes(expert_ids.reshape(2, TOK // 2, 2), 1, 2),
    )
    return section_out.reshape(tokens.shape), section_grad.reshape(tokens.shape)


def solution(mesh):
    in_specs = (
        P("pipe", None, "expert", None),
        P("pipe", None, "expert", None),
        P("pipe", None),
        P("pipe", None, None),
        P("pipe", "expert", None, "dp"),
        P("pipe", "expert", None, "dp"),
        P("pipe", "expert", "dp", None),
        P("pipe", None, "expert", None),
    )
    out_specs = (P("pipe", None, "expert", None), P("pipe", None, "expert", None))
    return jax.shard_map(shards, mesh=mesh, in_specs=in_specs, out_specs=out_specs, check_vma=False)
```

```python
import jax
import jax.numpy as jnp
from jax import lax
from jax.experimental import pallas as pl
from jax.experimental.pallas import tpu as pltpu
from jax.sharding import PartitionSpec as P

MESH = pl.DeviceIdType.MESH
F32 = jnp.float32
BF16 = jnp.bfloat16
HIGHEST = lax.Precision.HIGHEST

route_scale = 2.5
norm_eps = 1e-06

D = 3584
HID = 256
TOK = 128
ROWS = 256
HALF = D // 2
QUART = D // 4
PIECES = ((0, 0, 512), (0, 512, 384), (1, 0, 512), (1, 512, 384))
COUNT = len(PIECES)


def dot(a, b):
    return jnp.dot(a, b, preferred_element_type=F32)


def dot_nt(a, b, precision=None):
    return lax.dot_general(
        a, b, (((1,), (1,)), ((), ())), preferred_element_type=F32, precision=precision
    )


def iota(shape, dim):
    return lax.broadcasted_iota(jnp.int32, shape, dim)


def at128(start, size):
    return pl.ds(pl.multiple_of(start, 128), size)


def at16(start, size):
    return pl.ds(pl.multiple_of(start, 16), size)


def at8(start, size):
    return pl.ds(pl.multiple_of(start, 8), size)


def split(value):
    high = value.astype(BF16)
    return high, (value - high.astype(F32)).astype(BF16)


def kernel(
    tok_h,
    cot_h,
    gain_h,
    rout_h,
    wg_h,
    wu_h,
    wd_h,
    ids_h,
    out_v,
    grad_v,
    ids,
    gain,
    rout,
    hid,
    cot,
    nrm,
    wg,
    wu,
    wd,
    sel,
    com,
    cwh,
    cwl,
    inv_s,
    log_s,
    send,
    full,
    act_g,
    gv,
    uv,
    act,
    gg,
    ug,
    sc,
    scs,
    scr,
    lsem,
    d_s,
    d_r,
    f_s,
    f_r,
    s_s,
    s_r,
    e_s,
    e_r,
    p_s,
    p_r,
    r_s,
    r_r,
    a_s,
    a_r,
    c_s,
    c_r,
    x_s,
    x_r,
    *piece_refs,
):
    bufs = [piece_refs[i * 12 : (i + 1) * 12] for i in range(COUNT)]

    px = lax.axis_index("pipe")
    ex = lax.axis_index("expert")
    dx = lax.axis_index("dp")
    y = ex // 4
    zh = ex % 4
    zl = dx // 2
    c = dx % 2
    near = (zh + 2 * zl + 3) % 4
    far = (zh + 2) % 4
    opp = (zh + 5 - 2 * zl) % 4
    me = zh * 4 + y
    other = 1 - zl
    ys = [(y + dy) % 4 for dy in range(4)]
    yb = [(y + 4 - dy) % 4 for dy in range(4)]

    def dev(zh_, y_, zl_, c_):
        return (px, y_ * 4 + zh_, zl_ * 2 + c_)

    sibling = dev(zh, y, zl, 1 - c)
    partner = dev(zh, y, other, c)
    diagonal = dev(zh, y, other, 1 - c)
    after = ((px + 1) % 4, ex, dx)
    before = ((px + 3) % 4, ex, dx)

    def remote(src, dst, ssem, rsem, device):
        copy = pltpu.make_async_remote_copy(
            src_ref=src,
            dst_ref=dst,
            send_sem=ssem,
            recv_sem=rsem,
            device_id=device,
            device_id_type=MESH,
        )
        copy.start()
        return copy

    def take(ref, sem):
        pltpu.make_async_copy(ref, ref, sem).wait()

    barrier = pltpu.get_barrier_semaphore()
    greet = []
    for dy in (2, 1, 3, 0):
        greet += [
            dev(far, ys[dy], other, c),
            dev(near, ys[dy], zl, c),
            dev(opp, ys[dy], zl, c),
            dev(near, ys[dy], other, c),
        ]
        if dy:
            greet.append(dev(zh, ys[dy], zl, c))
    greet += [after, before, partner, diagonal, sibling]
    for device in greet:
        pl.semaphore_signal(barrier, inc=1, device_id=device, device_id_type=MESH)

    names = (ids, hid, gain, cot, wg, wu, wd, rout)
    sources = (ids_h, tok_h, gain_h, cot_h, wg_h, wu_h, wd_h, rout_h)
    loads = [
        pltpu.make_async_copy(a, b, lsem.at[i]) for i, (a, b) in enumerate(zip(sources, names))
    ]
    for load in loads[:3]:
        load.start()
    loads[0].wait()

    slot = iota((ROWS, TOK), 0)
    token = iota((ROWS, TOK), 1)
    slot_e = ((slot >> 4) & 3) * 4 + (slot >> 6)
    first = jnp.concatenate([ids[0, 0:1, :], ids[1, 0:1, :]], axis=1)
    second = jnp.concatenate([ids[0, 1:2, :], ids[1, 1:2, :]], axis=1)
    named = ((first == slot_e) | (second == slot_e)) & ((token >> 6) == ((slot >> 3) & 1))
    named = jnp.where(named, 1.0, 0.0)
    earlier = jnp.where(iota((TOK, TOK), 0) < iota((TOK, TOK), 1), 1.0, 0.0).astype(BF16)
    rank = dot(named.astype(BF16), earlier)
    picks = jnp.where(rank == (slot & 7).astype(F32), named, 0.0)
    sel[...] = picks.astype(BF16)

    half = c * HALF
    loads[1].wait()
    for load in loads[3:]:
        load.start()
    total = jnp.zeros((TOK, 1), F32)
    for i in range(4):
        part = hid[:, i * QUART : (i + 1) * QUART].astype(F32)
        total = total + jnp.sum(part * part, axis=1, keepdims=True)
    inv_s[...] = lax.rsqrt(total / D + norm_eps)

    def norm(start):
        for i in range(2):
            cols = at128(start + i * QUART, QUART)
            nrm[:, cols] = (hid[:, cols].astype(F32) * inv_s[...] * gain[:, cols]).astype(BF16)

    def gather(k, source):
        for i in range(2):
            send[k, :, i * QUART : (i + 1) * QUART] = dot(
                sel[...], source[:, at128(half + i * QUART, QUART)]
            ).astype(BF16)

    loads[2].wait()
    norm(half)
    gather(0, nrm)
    pl.semaphore_wait(barrier, len(greet))

    mine = at16(me * 16, 16)

    def send_near(k, dy):
        rows = at16((near * 4 + ys[dy]) * 16, 16)
        return remote(
            send.at[k, rows, :],
            full.at[k, mine, at128(half, HALF)],
            d_s.at[k],
            d_r.at[k, dy],
            dev(near, ys[dy], other, c),
        )

    def send_far(k, dy):
        rows = at16((far * 4 + ys[dy]) * 16, 16)
        return remote(
            send.at[k, rows, at128(zl * QUART, QUART)],
            full.at[k, mine, at128(half + zl * QUART, QUART)],
            d_s.at[k],
            d_r.at[k, 4 + dy],
            dev(far, ys[dy], other, c),
        )

    def send_own(k, dy):
        rows = at16((zh * 4 + ys[dy]) * 16, 16)
        return remote(
            send.at[k, rows, :],
            full.at[k, mine, at128(half, HALF)],
            d_s.at[k],
            d_r.at[k, 8],
            dev(zh, ys[dy], zl, c),
        )

    sent_x = [send_near(0, dy) for dy in range(4)]
    sent_x += [send_far(0, dy) for dy in range(4)]
    sent_x += [send_own(0, dy) for dy in range(1, 4)]
    full[0, mine, at128(half, HALF)] = send[0, mine, :]
    loads[3].wait()
    gather(1, cot)
    full[1, mine, at128(half, HALF)] = send[1, mine, :]

    def forward_near(k, sent):
        for dy in range(4):
            sent[dy].wait_recv()
            block = full.at[k, at16((near * 4 + yb[dy]) * 16, 16), at128(half, HALF)]
            remote(block, block, f_s.at[k], f_r.at[k, 0], partner)

    def forward_far(k, sent):
        for dy in range(4):
            sent[4 + dy].wait_recv()
            block = full.at[
                k,
                at16((far * 4 + yb[dy]) * 16, 16),
                at128(half + other * QUART, QUART),
            ]
            remote(block, block, f_s.at[k], f_r.at[k, 1], partner)

    def to_sibling(k, zh_):
        block = full.at[k, at16(zh_ * 64, 64), at128(half, HALF)]
        remote(block, block, s_s.at[k], s_r.at[k], sibling)

    def share_own(k):
        take(full.at[k, at16(zh * 64, 48), at128(half, HALF)], d_r.at[k, 8])
        to_sibling(k, zh)

    def share_opp(k):
        take(full.at[k, at16(opp * 64, 64), at128(half, HALF)], f_r.at[k, 0])
        to_sibling(k, opp)

    def share_far(k):
        take(full.at[k, at16(far * 64, 64), at128(half + zl * QUART, QUART)], f_r.at[k, 1])
        to_sibling(k, far)

    theirs = (1 - c) * HALF

    def complete(k):
        take(full.at[k, :, at128(theirs, HALF)], s_r.at[k])

    sent_u = [send_near(1, dy) for dy in range(4)]
    sent_u += [send_far(1, dy) for dy in range(4)]
    sent_u += [send_own(1, dy) for dy in range(1, 4)]
    forward_near(0, sent_x)
    to_sibling(0, near)
    forward_far(0, sent_x)
    share_own(0)

    com[...] = picks.T
    loads[7].wait()
    norm((1 - c) * HALF)
    log_s[...] = dot_nt(nrm[...], rout[...])
    spread = iota((16, ROWS), 1)
    spread = jnp.where(
        ((spread >> 4) & 3) * 4 + (spread >> 6) == iota((16, ROWS), 0), 1.0, 0.0
    )

    def chosen_parts():
        mask = dot_nt(com[...].astype(BF16), spread.astype(BF16))
        sig = jax.nn.sigmoid(log_s[...])
        csum = jnp.sum(mask * sig, axis=1, keepdims=True)
        return mask, sig, csum, route_scale * sig * mask / csum

    mask, sig, csum, w16 = chosen_parts()
    w_high, w_low = split(w16)
    cwh[...] = (dot(w_high, spread.astype(BF16)) * com[...]).astype(BF16)
    cwl[...] = (dot(w_low, spread.astype(BF16)) * com[...]).astype(BF16)

    share_opp(0)
    share_far(0)
    forward_near(1, sent_u)
    to_sibling(1, near)
    for load in loads[4:7]:
        load.wait()
    complete(0)

    gv[...] = dot(full[0], wg[...])
    uv[...] = dot(full[0], wu[...])
    g = gv[...]
    act[...] = (g * jax.nn.sigmoid(g) * uv[...]).astype(BF16)

    def down(cols):
        return dot(act[...], wd[:, cols])

    def back(cols):
        return dot_nt(gg[...], wg[cols, :]) + dot_nt(ug[...], wu[cols, :])

    terms = (down, back)
    def swap(p):
        k, off, w = PIECES[p]
        es, er = bufs[p][0], bufs[p][2]
        for i in range(2):
            es[:, i * w : (i + 1) * w] = terms[k](at128(theirs + i * QUART + off, w)).astype(BF16)
        return remote(es, er, e_s.at[p], e_r.at[p], sibling)

    def keep(p):
        k, off, w = PIECES[p]
        eo = bufs[p][1]
        for i in range(2):
            eo[:, i * w : (i + 1) * w] = terms[k](at128(half + i * QUART + off, w))

    def pair_sum(p, swapped):
        w = PIECES[p][2]
        es, eo, er, cp, pa, pb, pc = bufs[p][:7]
        swapped.wait_recv()

        def add(zh_):
            rows = at16(zh_ * 64, 64)
            cp[rows, :] = (eo[rows, :] + er[rows, :].astype(F32)).astype(BF16)
            return rows

        rows = add(far)
        copies = [
            remote(cp.at[rows, at128(zl * w, w)], pb, p_s.at[p], p_r.at[p, 0], partner)
        ]
        rows = add(opp)
        copies.append(remote(cp.at[rows, :], pa, p_s.at[p], p_r.at[p, 1], partner))
        rows = add(zh)
        copies.append(
            remote(cp.at[rows, at128(other * w, w)], pc, p_s.at[p], p_r.at[p, 2], partner)
        )
        add(near)
        return copies

    def give_back(p, pair):
        w = PIECES[p][2]
        cp, pa, pb, pc, fa, fb, fc, ret = bufs[p][3:11]

        def give(src, zh_, dy, zl_):
            remote(src, ret.at[mine, :], r_s.at[p], r_r.at[p], dev(zh_, ys[dy], zl_, c))

        pair[0].wait_recv()
        fb[...] = (
            cp[at16(far * 64, 64), at128(other * w, w)].astype(F32) + pb[...].astype(F32)
        ).astype(BF16)
        for dy in range(4):
            give(fb.at[at16(ys[dy] * 16, 16), :], far, dy, other)
        pair[1].wait_recv()
        fa[...] = (cp[at16(near * 64, 64), :].astype(F32) + pa[...].astype(F32)).astype(BF16)
        for dy in range(4):
            rows = at16(ys[dy] * 16, 16)
            give(fa.at[rows, at128(zl * w, w)], near, dy, zl)
            give(fa.at[rows, at128(other * w, w)], near, dy, other)
        pair[2].wait_recv()
        fc[...] = (
            cp[at16(zh * 64, 64), at128(zl * w, w)].astype(F32) + pc[...].astype(F32)
        ).astype(BF16)
        for dy in range(1, 4):
            give(fc.at[at16(ys[dy] * 16, 16), :], zh, dy, zl)
        ret[mine, :] = fc[at16(y * 16, 16), :]

    swaps = [swap(0), swap(1)]
    keep(0)
    forward_far(1, sent_u)
    share_own(1)
    pairs = [pair_sum(0, swaps[0])]
    share_opp(1)
    keep(1)
    pairs.append(pair_sum(1, swaps[1]))
    share_far(1)
    complete(1)

    act_g[...] = dot_nt(full[1], wd[...])
    g, u, a = gv[...], uv[...], act_g[...]
    sigma = jax.nn.sigmoid(g)
    gg[...] = (a * u * sigma * (1.0 + g * (1.0 - sigma))).astype(BF16)
    ug[...] = (a * g * sigma).astype(BF16)
    swaps += [swap(2), swap(3)]

    ones = jnp.ones((8, HID), F32)
    w_row = dot_nt(ones, act[...].astype(F32) * act_g[...], HIGHEST)
    n_row = dot_nt(
        ones, gg[...].astype(F32) * gv[...] + ug[...].astype(F32) * uv[...], HIGHEST
    )
    line = iota((8, ROWS), 0)
    sc[dx] = jnp.where(line == 0, w_row, jnp.where(line == 1, n_row, 0.0))
    for device in (sibling, partner, diagonal):
        remote(sc.at[dx], sc.at[dx], a_s.at[0], a_r.at[0], device)
    keep(2)
    give_back(0, pairs[0])
    pairs.append(pair_sum(2, swaps[2]))
    keep(3)
    give_back(1, pairs[1])
    pairs.append(pair_sum(3, swaps[3]))

    take(sc.at[0:3], a_r.at[0])
    scs[...] = (sc[0] + sc[1]) + (sc[2] + sc[3])
    own_notes = at8(me * 8, 8)
    for dy in range(4):
        for zh_, zl_ in ((near, other), (near, zl), (far, other)) + (((zh, zl),) if dy else ()):
            remote(
                scs.at[:, at128((zh_ // 2) * 128, 128)],
                scr.at[own_notes, :],
                c_s.at[0],
                c_r.at[0],
                dev(zh_, ys[dy], zl_, c),
            )
    scr[own_notes, :] = scs[:, at128((zh // 2) * 128, 128)]

    quarter = half + zl * QUART
    results = (out_v, grad_v)

    def combine(p):
        ret = bufs[p][10]
        take(ret.at[0:240, :], r_r.at[p])
        return dot(cwh[...], ret[...]) + dot(cwl[...], ret[...])

    def ship(p, value, device):
        k, off, w = PIECES[p]
        fin = bufs[p][11]
        fin[...] = value.astype(BF16)
        return remote(
            fin, results[k].at[:, at128(quarter + off, w)], x_s.at[p], x_r.at[p, 0], device
        )

    def pass_on(p, shift):
        k, off, w = PIECES[p]
        shift.wait_recv()
        block = results[k].at[:, at128(quarter + off, w)]
        remote(block, block, x_s.at[p], x_r.at[p, 2], sibling)
        return remote(block, block, x_s.at[p], x_r.at[p, 1], partner)

    def pass_last(p, passed):
        k, off, w = PIECES[p]
        passed.wait_recv()
        block = results[k].at[:, at128(half + other * QUART + off, w)]
        remote(block, block, x_s.at[p], x_r.at[p, 2], sibling)

    def forward_result(p):
        k, off, w = PIECES[p]
        return hid[:, at128(quarter + off, w)].astype(F32) + combine(p)

    shifts = [ship(0, forward_result(0), after)]
    shifts.append(ship(1, forward_result(1), after))
    passed = [pass_on(0, shifts[0])]
    give_back(2, pairs[2])
    passed.append(pass_on(1, shifts[1]))
    give_back(3, pairs[3])

    take(scr.at[0:120, :], c_r.at[0])
    lane_at = (me % 8) * 16
    row, col = iota((128, ROWS), 0), iota((128, ROWS), 1)
    turn = jnp.where(row == lane_at + (col & 15), 1.0, 0.0)
    moved = jnp.dot(scr[...], turn, precision=HIGHEST, preferred_element_type=F32)
    own_row = (row >> 3) == (col >> 4)
    w_row = jnp.sum(jnp.where(own_row & ((row & 7) == 0), moved, 0.0), axis=0, keepdims=True)
    n_row = jnp.sum(jnp.where(own_row & ((row & 7) == 1), moved, 0.0), axis=0, keepdims=True)
    mask, sig, csum, w16 = chosen_parts()
    weight_grad = dot_nt(com[...] * w_row, spread, HIGHEST)
    total = jnp.sum(weight_grad * w16, axis=1, keepdims=True)
    logit_grad = (route_scale * weight_grad - total) / csum * sig * (1.0 - sig) * mask
    weighted = cwh[...].astype(F32) + cwl[...].astype(F32)
    inner = jnp.sum(weighted * n_row, axis=1, keepdims=True) + jnp.sum(
        logit_grad * log_s[...], axis=1, keepdims=True
    )
    l_high, l_low = split(logit_grad)
    inverse = inv_s[...]
    pull = inverse * inverse * inner / D

    def gradient(p):
        k, off, w = PIECES[p]
        cols = at128(quarter + off, w)
        routers = rout[:, cols]
        normed_grad = combine(p) + (dot(l_high, routers) + dot(l_low, routers))
        return (
            cot[:, cols].astype(F32)
            + inverse * gain[:, cols] * normed_grad
            - hid[:, cols].astype(F32) * pull
        )

    shifts.append(ship(2, gradient(2), before))
    pass_last(0, passed[0])
    pass_last(1, passed[1])
    shifts.append(ship(3, gradient(3), before))
    passed.append(pass_on(2, shifts[2]))
    passed.append(pass_on(3, shifts[3]))
    pass_last(2, passed[2])
    pass_last(3, passed[3])
    for p in range(COUNT):
        take(bufs[p][10], x_r.at[p, 2])
    for k in range(2):
        take(send.at[k, 0:144, :], d_s.at[k])
        take(send.at[k, 0:96, :], f_s.at[k])
        take(send.at[k], s_s.at[k])
    for p in range(COUNT):
        es, cp, ret = bufs[p][0], bufs[p][3], bufs[p][10]
        take(es, e_s.at[p])
        take(cp.at[0:128, :], p_s.at[p])
        take(ret.at[0:240, :], r_s.at[p])
        take(es, x_s.at[p])
    take(sc.at[0:3], a_s.at[0])
    take(scr.at[0:120, :], c_s.at[0])


def shards(tokens, cotangent, gain, router, w_gate, w_up, w_down, expert_ids):
    anywhere = pl.BlockSpec(memory_space=pl.ANY)
    vmem = pl.BlockSpec(memory_space=pltpu.VMEM)

    def buf(*shape, dtype=BF16):
        return pltpu.VMEM(shape, dtype)

    def sems(*shape):
        return pltpu.SemaphoreType.DMA(shape)

    scratch = [
        buf(2, 2, TOK // 2, dtype=jnp.int32),
        buf(1, D, dtype=F32),
        buf(16, D),
        buf(TOK, D),
        buf(TOK, D),
        buf(TOK, D),
        buf(D, HID),
        buf(D, HID),
        buf(HID, D),
        buf(ROWS, TOK),
        buf(TOK, ROWS, dtype=F32),
        buf(TOK, ROWS),
        buf(TOK, ROWS),
        buf(TOK, 1, dtype=F32),
        buf(TOK, 16, dtype=F32),
        buf(2, ROWS, HALF),
        buf(2, ROWS, D),
        buf(ROWS, HID, dtype=F32),
        buf(ROWS, HID, dtype=F32),
        buf(ROWS, HID, dtype=F32),
        buf(ROWS, HID),
        buf(ROWS, HID),
        buf(ROWS, HID),
        buf(4, 8, ROWS, dtype=F32),
        buf(8, ROWS, dtype=F32),
        buf(128, 128, dtype=F32),
        sems(8),
        sems(2),
        sems(2, 9),
        sems(2),
        sems(2, 2),
        sems(2),
        sems(2),
        sems(COUNT),
        sems(COUNT),
        sems(COUNT),
        sems(COUNT, 3),
        sems(COUNT),
        sems(COUNT),
        sems(1),
        sems(1),
        sems(1),
        sems(1),
        sems(COUNT),
        sems(COUNT, 3),
    ]
    for _, _, w in PIECES:
        scratch += [
            buf(ROWS, 2 * w),
            buf(ROWS, 2 * w, dtype=F32),
            buf(ROWS, 2 * w),
            buf(ROWS, 2 * w),
            buf(64, 2 * w),
            buf(64, w),
            buf(64, w),
            buf(64, 2 * w),
            buf(64, w),
            buf(64, w),
            buf(ROWS, w),
            buf(TOK, w),
        ]
    out = pltpu.VMEM((TOK, D), BF16)
    section_out, section_grad = pl.pallas_call(
        kernel,
        out_shape=(out, out),
        in_specs=[anywhere] * 8,
        out_specs=(vmem, vmem),
        scratch_shapes=scratch,
        compiler_params=pltpu.CompilerParams(
            collective_id=0, has_side_effects=True, vmem_limit_bytes=56 * 1024 * 1024
        ),
    )(
        tokens.reshape(TOK, D),
        cotangent.reshape(TOK, D),
        gain,
        jnp.swapaxes(router.reshape(D, 16), 0, 1),
        w_gate.reshape(D, HID),
        w_up.reshape(D, HID),
        w_down.reshape(HID, D),
        jnp.swapaxes(expert_ids.reshape(2, TOK // 2, 2), 1, 2),
    )
    return section_out.reshape(tokens.shape), section_grad.reshape(tokens.shape)


def solution(mesh):
    in_specs = (
        P("pipe", None, "expert", None),
        P("pipe", None, "expert", None),
        P("pipe", None),
        P("pipe", None, None),
        P("pipe", "expert", None, "dp"),
        P("pipe", "expert", None, "dp"),
        P("pipe", "expert", "dp", None),
        P("pipe", None, "expert", None),
    )
    out_specs = (P("pipe", None, "expert", None), P("pipe", None, "expert", None))
    return jax.shard_map(shards, mesh=mesh, in_specs=in_specs, out_specs=out_specs, check_vma=False)
```

```python
import jax
import jax.numpy as jnp
from jax import lax
from jax.experimental import pallas as pl
from jax.experimental.pallas import tpu as pltpu
from jax.sharding import PartitionSpec as P

MESH = pl.DeviceIdType.MESH
F32 = jnp.float32
BF16 = jnp.bfloat16
HIGHEST = lax.Precision.HIGHEST

route_scale = 2.5
norm_eps = 1e-06

D = 3584
HID = 256
TOK = 128
ROWS = 256
HALF = D // 2
QUART = D // 4
PIECES = ((0, 0, 512), (0, 512, 384), (1, 0, 640), (1, 640, 256))
COUNT = len(PIECES)


def dot(a, b):
    return jnp.dot(a, b, preferred_element_type=F32)


def dot_nt(a, b, precision=None):
    return lax.dot_general(
        a, b, (((1,), (1,)), ((), ())), preferred_element_type=F32, precision=precision
    )


def iota(shape, dim):
    return lax.broadcasted_iota(jnp.int32, shape, dim)


def at128(start, size):
    return pl.ds(pl.multiple_of(start, 128), size)


def at16(start, size):
    return pl.ds(pl.multiple_of(start, 16), size)


def at8(start, size):
    return pl.ds(pl.multiple_of(start, 8), size)


def split(value):
    high = value.astype(BF16)
    return high, (value - high.astype(F32)).astype(BF16)


def kernel(
    tok_h,
    cot_h,
    gain_h,
    rout_h,
    wg_h,
    wu_h,
    wd_h,
    ids_h,
    out_v,
    grad_v,
    ids,
    gain,
    rout,
    hid,
    cot,
    nrm,
    wg,
    wu,
    wd,
    sel,
    com,
    cwh,
    cwl,
    inv_s,
    log_s,
    send,
    full,
    act_g,
    gv,
    uv,
    act,
    gg,
    ug,
    sc,
    scs,
    scr,
    lsem,
    d_s,
    d_r,
    f_s,
    f_r,
    s_s,
    s_r,
    e_s,
    e_r,
    p_s,
    p_r,
    r_s,
    r_r,
    a_s,
    a_r,
    c_s,
    c_r,
    x_s,
    x_r,
    *piece_refs,
):
    bufs = [piece_refs[i * 12 : (i + 1) * 12] for i in range(COUNT)]

    px = lax.axis_index("pipe")
    ex = lax.axis_index("expert")
    dx = lax.axis_index("dp")
    y = ex // 4
    zh = ex % 4
    zl = dx // 2
    c = dx % 2
    near = (zh + 2 * zl + 3) % 4
    far = (zh + 2) % 4
    opp = (zh + 5 - 2 * zl) % 4
    me = zh * 4 + y
    other = 1 - zl
    ys = [(y + dy) % 4 for dy in range(4)]
    yb = [(y + 4 - dy) % 4 for dy in range(4)]

    def dev(zh_, y_, zl_, c_):
        return (px, y_ * 4 + zh_, zl_ * 2 + c_)

    sibling = dev(zh, y, zl, 1 - c)
    partner = dev(zh, y, other, c)
    diagonal = dev(zh, y, other, 1 - c)
    after = ((px + 1) % 4, ex, dx)
    before = ((px + 3) % 4, ex, dx)

    def remote(src, dst, ssem, rsem, device):
        copy = pltpu.make_async_remote_copy(
            src_ref=src,
            dst_ref=dst,
            send_sem=ssem,
            recv_sem=rsem,
            device_id=device,
            device_id_type=MESH,
        )
        copy.start()
        return copy

    def take(ref, sem):
        pltpu.make_async_copy(ref, ref, sem).wait()

    barrier = pltpu.get_barrier_semaphore()
    greet = []
    for dy in (2, 1, 3, 0):
        greet += [
            dev(far, ys[dy], other, c),
            dev(near, ys[dy], zl, c),
            dev(opp, ys[dy], zl, c),
            dev(near, ys[dy], other, c),
        ]
        if dy:
            greet.append(dev(zh, ys[dy], zl, c))
    greet += [after, before, partner, diagonal, sibling]
    for device in greet:
        pl.semaphore_signal(barrier, inc=1, device_id=device, device_id_type=MESH)

    names = (ids, hid, gain, cot, wg, wu, wd, rout)
    sources = (ids_h, tok_h, gain_h, cot_h, wg_h, wu_h, wd_h, rout_h)
    loads = [
        pltpu.make_async_copy(a, b, lsem.at[i]) for i, (a, b) in enumerate(zip(sources, names))
    ]
    for load in loads[:3]:
        load.start()
    loads[0].wait()

    slot = iota((ROWS, TOK), 0)
    token = iota((ROWS, TOK), 1)
    slot_e = ((slot >> 4) & 3) * 4 + (slot >> 6)
    first = jnp.concatenate([ids[0, 0:1, :], ids[1, 0:1, :]], axis=1)
    second = jnp.concatenate([ids[0, 1:2, :], ids[1, 1:2, :]], axis=1)
    named = ((first == slot_e) | (second == slot_e)) & ((token >> 6) == ((slot >> 3) & 1))
    named = jnp.where(named, 1.0, 0.0)
    earlier = jnp.where(iota((TOK, TOK), 0) < iota((TOK, TOK), 1), 1.0, 0.0).astype(BF16)
    rank = dot(named.astype(BF16), earlier)
    picks = jnp.where(rank == (slot & 7).astype(F32), named, 0.0)
    sel[...] = picks.astype(BF16)

    half = c * HALF
    loads[1].wait()
    for load in loads[3:]:
        load.start()
    total = jnp.zeros((TOK, 1), F32)
    for i in range(4):
        part = hid[:, i * QUART : (i + 1) * QUART].astype(F32)
        total = total + jnp.sum(part * part, axis=1, keepdims=True)
    inv_s[...] = lax.rsqrt(total / D + norm_eps)

    def norm(start):
        for i in range(2):
            cols = at128(start + i * QUART, QUART)
            nrm[:, cols] = (hid[:, cols].astype(F32) * inv_s[...] * gain[:, cols]).astype(BF16)

    def gather(k, source):
        for i in range(2):
            send[k, :, i * QUART : (i + 1) * QUART] = dot(
                sel[...], source[:, at128(half + i * QUART, QUART)]
            ).astype(BF16)

    loads[2].wait()
    norm(half)
    gather(0, nrm)
    pl.semaphore_wait(barrier, len(greet))

    mine = at16(me * 16, 16)

    def send_near(k, dy):
        rows = at16((near * 4 + ys[dy]) * 16, 16)
        return remote(
            send.at[k, rows, :],
            full.at[k, mine, at128(half, HALF)],
            d_s.at[k],
            d_r.at[k, dy],
            dev(near, ys[dy], other, c),
        )

    def send_far(k, dy):
        rows = at16((far * 4 + ys[dy]) * 16, 16)
        return remote(
            send.at[k, rows, at128(zl * QUART, QUART)],
            full.at[k, mine, at128(half + zl * QUART, QUART)],
            d_s.at[k],
            d_r.at[k, 4 + dy],
            dev(far, ys[dy], other, c),
        )

    def send_own(k, dy):
        rows = at16((zh * 4 + ys[dy]) * 16, 16)
        return remote(
            send.at[k, rows, :],
            full.at[k, mine, at128(half, HALF)],
            d_s.at[k],
            d_r.at[k, 8],
            dev(zh, ys[dy], zl, c),
        )

    sent_x = [send_near(0, dy) for dy in range(4)]
    sent_x += [send_far(0, dy) for dy in range(4)]
    sent_x += [send_own(0, dy) for dy in range(1, 4)]
    full[0, mine, at128(half, HALF)] = send[0, mine, :]
    loads[3].wait()
    gather(1, cot)
    full[1, mine, at128(half, HALF)] = send[1, mine, :]

    def forward_near(k, sent):
        for dy in range(4):
            sent[dy].wait_recv()
            block = full.at[k, at16((near * 4 + yb[dy]) * 16, 16), at128(half, HALF)]
            remote(block, block, f_s.at[k], f_r.at[k, 0], partner)

    def forward_far(k, sent):
        for dy in range(4):
            sent[4 + dy].wait_recv()
            block = full.at[
                k,
                at16((far * 4 + yb[dy]) * 16, 16),
                at128(half + other * QUART, QUART),
            ]
            remote(block, block, f_s.at[k], f_r.at[k, 1], partner)

    def to_sibling(k, zh_):
        block = full.at[k, at16(zh_ * 64, 64), at128(half, HALF)]
        remote(block, block, s_s.at[k], s_r.at[k], sibling)

    def share_own(k):
        take(full.at[k, at16(zh * 64, 48), at128(half, HALF)], d_r.at[k, 8])
        to_sibling(k, zh)

    def share_opp(k):
        take(full.at[k, at16(opp * 64, 64), at128(half, HALF)], f_r.at[k, 0])
        to_sibling(k, opp)

    def share_far(k):
        take(full.at[k, at16(far * 64, 64), at128(half + zl * QUART, QUART)], f_r.at[k, 1])
        to_sibling(k, far)

    theirs = (1 - c) * HALF

    def complete(k):
        take(full.at[k, :, at128(theirs, HALF)], s_r.at[k])

    sent_u = [send_near(1, dy) for dy in range(4)]
    sent_u += [send_far(1, dy) for dy in range(4)]
    sent_u += [send_own(1, dy) for dy in range(1, 4)]
    forward_near(0, sent_x)
    to_sibling(0, near)
    forward_far(0, sent_x)
    share_own(0)

    com[...] = picks.T
    loads[7].wait()
    norm((1 - c) * HALF)
    log_s[...] = dot_nt(nrm[...], rout[...])
    spread = iota((16, ROWS), 1)
    spread = jnp.where(
        ((spread >> 4) & 3) * 4 + (spread >> 6) == iota((16, ROWS), 0), 1.0, 0.0
    )

    def chosen_parts():
        mask = dot_nt(com[...].astype(BF16), spread.astype(BF16))
        sig = jax.nn.sigmoid(log_s[...])
        csum = jnp.sum(mask * sig, axis=1, keepdims=True)
        return mask, sig, csum, route_scale * sig * mask / csum

    mask, sig, csum, w16 = chosen_parts()
    w_high, w_low = split(w16)
    cwh[...] = (dot(w_high, spread.astype(BF16)) * com[...]).astype(BF16)
    cwl[...] = (dot(w_low, spread.astype(BF16)) * com[...]).astype(BF16)

    share_opp(0)
    share_far(0)
    forward_near(1, sent_u)
    to_sibling(1, near)
    for load in loads[4:7]:
        load.wait()
    complete(0)

    gv[...] = dot(full[0], wg[...])
    uv[...] = dot(full[0], wu[...])
    g = gv[...]
    act[...] = (g * jax.nn.sigmoid(g) * uv[...]).astype(BF16)

    def down(cols):
        return dot(act[...], wd[:, cols])

    def back(cols):
        return dot_nt(gg[...], wg[cols, :]) + dot_nt(ug[...], wu[cols, :])

    terms = (down, back)
    def swap(p):
        k, off, w = PIECES[p]
        es, er = bufs[p][0], bufs[p][2]
        for i in range(2):
            es[:, i * w : (i + 1) * w] = terms[k](at128(theirs + i * QUART + off, w)).astype(BF16)
        return remote(es, er, e_s.at[p], e_r.at[p], sibling)

    def keep(p):
        k, off, w = PIECES[p]
        eo = bufs[p][1]
        for i in range(2):
            eo[:, i * w : (i + 1) * w] = terms[k](at128(half + i * QUART + off, w))

    def pair_sum(p, swapped):
        w = PIECES[p][2]
        es, eo, er, cp, pa, pb, pc = bufs[p][:7]
        swapped.wait_recv()

        def add(zh_):
            rows = at16(zh_ * 64, 64)
            cp[rows, :] = (eo[rows, :] + er[rows, :].astype(F32)).astype(BF16)
            return rows

        rows = add(far)
        copies = [
            remote(cp.at[rows, at128(zl * w, w)], pb, p_s.at[p], p_r.at[p, 0], partner)
        ]
        rows = add(opp)
        copies.append(remote(cp.at[rows, :], pa, p_s.at[p], p_r.at[p, 1], partner))
        rows = add(zh)
        copies.append(
            remote(cp.at[rows, at128(other * w, w)], pc, p_s.at[p], p_r.at[p, 2], partner)
        )
        add(near)
        return copies

    def give_back(p, pair):
        w = PIECES[p][2]
        cp, pa, pb, pc, fa, fb, fc, ret = bufs[p][3:11]

        def give(src, zh_, dy, zl_):
            remote(src, ret.at[mine, :], r_s.at[p], r_r.at[p], dev(zh_, ys[dy], zl_, c))

        pair[0].wait_recv()
        fb[...] = (
            cp[at16(far * 64, 64), at128(other * w, w)].astype(F32) + pb[...].astype(F32)
        ).astype(BF16)
        for dy in range(4):
            give(fb.at[at16(ys[dy] * 16, 16), :], far, dy, other)
        pair[1].wait_recv()
        fa[...] = (cp[at16(near * 64, 64), :].astype(F32) + pa[...].astype(F32)).astype(BF16)
        for dy in range(4):
            rows = at16(ys[dy] * 16, 16)
            give(fa.at[rows, at128(zl * w, w)], near, dy, zl)
            give(fa.at[rows, at128(other * w, w)], near, dy, other)
        pair[2].wait_recv()
        fc[...] = (
            cp[at16(zh * 64, 64), at128(zl * w, w)].astype(F32) + pc[...].astype(F32)
        ).astype(BF16)
        for dy in range(1, 4):
            give(fc.at[at16(ys[dy] * 16, 16), :], zh, dy, zl)
        ret[mine, :] = fc[at16(y * 16, 16), :]

    swaps = [swap(0), swap(1)]
    keep(0)
    forward_far(1, sent_u)
    share_own(1)
    pairs = [pair_sum(0, swaps[0])]
    share_opp(1)
    keep(1)
    pairs.append(pair_sum(1, swaps[1]))
    share_far(1)
    complete(1)

    act_g[...] = dot_nt(full[1], wd[...])
    g, u, a = gv[...], uv[...], act_g[...]
    sigma = jax.nn.sigmoid(g)
    gg[...] = (a * u * sigma * (1.0 + g * (1.0 - sigma))).astype(BF16)
    ug[...] = (a * g * sigma).astype(BF16)
    swaps += [swap(2), swap(3)]
    give_back(0, pairs[0])

    ones = jnp.ones((8, HID), F32)
    w_row = dot_nt(ones, act[...].astype(F32) * act_g[...], HIGHEST)
    n_row = dot_nt(
        ones, gg[...].astype(F32) * gv[...] + ug[...].astype(F32) * uv[...], HIGHEST
    )
    line = iota((8, ROWS), 0)
    sc[dx] = jnp.where(line == 0, w_row, jnp.where(line == 1, n_row, 0.0))
    for device in (sibling, partner, diagonal):
        remote(sc.at[dx], sc.at[dx], a_s.at[0], a_r.at[0], device)
    keep(2)
    pairs.append(pair_sum(2, swaps[2]))
    keep(3)
    give_back(1, pairs[1])
    pairs.append(pair_sum(3, swaps[3]))

    take(sc.at[0:3], a_r.at[0])
    scs[...] = (sc[0] + sc[1]) + (sc[2] + sc[3])
    own_notes = at8(me * 8, 8)
    for dy in range(4):
        for zh_, zl_ in ((near, other), (near, zl), (far, other)) + (((zh, zl),) if dy else ()):
            remote(
                scs.at[:, at128((zh_ // 2) * 128, 128)],
                scr.at[own_notes, :],
                c_s.at[0],
                c_r.at[0],
                dev(zh_, ys[dy], zl_, c),
            )
    scr[own_notes, :] = scs[:, at128((zh // 2) * 128, 128)]

    quarter = half + zl * QUART
    results = (out_v, grad_v)

    def combine(p):
        ret = bufs[p][10]
        take(ret.at[0:240, :], r_r.at[p])
        return dot(cwh[...], ret[...]) + dot(cwl[...], ret[...])

    def ship(p, value, device):
        k, off, w = PIECES[p]
        fin = bufs[p][11]
        fin[...] = value.astype(BF16)
        return remote(
            fin, results[k].at[:, at128(quarter + off, w)], x_s.at[p], x_r.at[p, 0], device
        )

    def pass_on(p, shift):
        k, off, w = PIECES[p]
        shift.wait_recv()
        block = results[k].at[:, at128(quarter + off, w)]
        remote(block, block, x_s.at[p], x_r.at[p, 2], sibling)
        return remote(block, block, x_s.at[p], x_r.at[p, 1], partner)

    def pass_last(p, passed):
        k, off, w = PIECES[p]
        passed.wait_recv()
        block = results[k].at[:, at128(half + other * QUART + off, w)]
        remote(block, block, x_s.at[p], x_r.at[p, 2], sibling)

    def forward_result(p):
        k, off, w = PIECES[p]
        return hid[:, at128(quarter + off, w)].astype(F32) + combine(p)

    shifts = [ship(0, forward_result(0), after)]
    shifts.append(ship(1, forward_result(1), after))
    passed = [pass_on(0, shifts[0])]
    give_back(2, pairs[2])
    passed.append(pass_on(1, shifts[1]))
    give_back(3, pairs[3])

    take(scr.at[0:120, :], c_r.at[0])
    lane_at = (me % 8) * 16
    row, col = iota((128, ROWS), 0), iota((128, ROWS), 1)
    turn = jnp.where(row == lane_at + (col & 15), 1.0, 0.0)
    moved = jnp.dot(scr[...], turn, precision=HIGHEST, preferred_element_type=F32)
    own_row = (row >> 3) == (col >> 4)
    w_row = jnp.sum(jnp.where(own_row & ((row & 7) == 0), moved, 0.0), axis=0, keepdims=True)
    n_row = jnp.sum(jnp.where(own_row & ((row & 7) == 1), moved, 0.0), axis=0, keepdims=True)
    mask, sig, csum, w16 = chosen_parts()
    weight_grad = dot_nt(com[...] * w_row, spread, HIGHEST)
    total = jnp.sum(weight_grad * w16, axis=1, keepdims=True)
    logit_grad = (route_scale * weight_grad - total) / csum * sig * (1.0 - sig) * mask
    weighted = cwh[...].astype(F32) + cwl[...].astype(F32)
    inner = jnp.sum(weighted * n_row, axis=1, keepdims=True) + jnp.sum(
        logit_grad * log_s[...], axis=1, keepdims=True
    )
    l_high, l_low = split(logit_grad)
    inverse = inv_s[...]
    pull = inverse * inverse * inner / D

    def gradient(p):
        k, off, w = PIECES[p]
        cols = at128(quarter + off, w)
        routers = rout[:, cols]
        normed_grad = combine(p) + (dot(l_high, routers) + dot(l_low, routers))
        return (
            cot[:, cols].astype(F32)
            + inverse * gain[:, cols] * normed_grad
            - hid[:, cols].astype(F32) * pull
        )

    shifts.append(ship(2, gradient(2), before))
    pass_last(0, passed[0])
    pass_last(1, passed[1])
    shifts.append(ship(3, gradient(3), before))
    passed.append(pass_on(2, shifts[2]))
    passed.append(pass_on(3, shifts[3]))
    pass_last(2, passed[2])
    pass_last(3, passed[3])
    for p in range(COUNT):
        take(bufs[p][10], x_r.at[p, 2])
    for k in range(2):
        take(send.at[k, 0:144, :], d_s.at[k])
        take(send.at[k, 0:96, :], f_s.at[k])
        take(send.at[k], s_s.at[k])
    for p in range(COUNT):
        es, cp, ret = bufs[p][0], bufs[p][3], bufs[p][10]
        take(es, e_s.at[p])
        take(cp.at[0:128, :], p_s.at[p])
        take(ret.at[0:240, :], r_s.at[p])
        take(es, x_s.at[p])
    take(sc.at[0:3], a_s.at[0])
    take(scr.at[0:120, :], c_s.at[0])


def shards(tokens, cotangent, gain, router, w_gate, w_up, w_down, expert_ids):
    anywhere = pl.BlockSpec(memory_space=pl.ANY)
    vmem = pl.BlockSpec(memory_space=pltpu.VMEM)

    def buf(*shape, dtype=BF16):
        return pltpu.VMEM(shape, dtype)

    def sems(*shape):
        return pltpu.SemaphoreType.DMA(shape)

    scratch = [
        buf(2, 2, TOK // 2, dtype=jnp.int32),
        buf(1, D, dtype=F32),
        buf(16, D),
        buf(TOK, D),
        buf(TOK, D),
        buf(TOK, D),
        buf(D, HID),
        buf(D, HID),
        buf(HID, D),
        buf(ROWS, TOK),
        buf(TOK, ROWS, dtype=F32),
        buf(TOK, ROWS),
        buf(TOK, ROWS),
        buf(TOK, 1, dtype=F32),
        buf(TOK, 16, dtype=F32),
        buf(2, ROWS, HALF),
        buf(2, ROWS, D),
        buf(ROWS, HID, dtype=F32),
        buf(ROWS, HID, dtype=F32),
        buf(ROWS, HID, dtype=F32),
        buf(ROWS, HID),
        buf(ROWS, HID),
        buf(ROWS, HID),
        buf(4, 8, ROWS, dtype=F32),
        buf(8, ROWS, dtype=F32),
        buf(128, 128, dtype=F32),
        sems(8),
        sems(2),
        sems(2, 9),
        sems(2),
        sems(2, 2),
        sems(2),
        sems(2),
        sems(COUNT),
        sems(COUNT),
        sems(COUNT),
        sems(COUNT, 3),
        sems(COUNT),
        sems(COUNT),
        sems(1),
        sems(1),
        sems(1),
        sems(1),
        sems(COUNT),
        sems(COUNT, 3),
    ]
    for _, _, w in PIECES:
        scratch += [
            buf(ROWS, 2 * w),
            buf(ROWS, 2 * w, dtype=F32),
            buf(ROWS, 2 * w),
            buf(ROWS, 2 * w),
            buf(64, 2 * w),
            buf(64, w),
            buf(64, w),
            buf(64, 2 * w),
            buf(64, w),
            buf(64, w),
            buf(ROWS, w),
            buf(TOK, w),
        ]
    out = pltpu.VMEM((TOK, D), BF16)
    section_out, section_grad = pl.pallas_call(
        kernel,
        out_shape=(out, out),
        in_specs=[anywhere] * 8,
        out_specs=(vmem, vmem),
        scratch_shapes=scratch,
        compiler_params=pltpu.CompilerParams(
            collective_id=0, has_side_effects=True, vmem_limit_bytes=56 * 1024 * 1024
        ),
    )(
        tokens.reshape(TOK, D),
        cotangent.reshape(TOK, D),
        gain,
        jnp.swapaxes(router.reshape(D, 16), 0, 1),
        w_gate.reshape(D, HID),
        w_up.reshape(D, HID),
        w_down.reshape(HID, D),
        jnp.swapaxes(expert_ids.reshape(2, TOK // 2, 2), 1, 2),
    )
    return section_out.reshape(tokens.shape), section_grad.reshape(tokens.shape)


def solution(mesh):
    in_specs = (
        P("pipe", None, "expert", None),
        P("pipe", None, "expert", None),
        P("pipe", None),
        P("pipe", None, None),
        P("pipe", "expert", None, "dp"),
        P("pipe", "expert", None, "dp"),
        P("pipe", "expert", "dp", None),
        P("pipe", None, "expert", None),
    )
    out_specs = (P("pipe", None, "expert", None), P("pipe", None, "expert", None))
    return jax.shard_map(shards, mesh=mesh, in_specs=in_specs, out_specs=out_specs, check_vma=False)
```

```python
import jax
import jax.numpy as jnp
from jax import lax
from jax.experimental import pallas as pl
from jax.experimental.pallas import tpu as pltpu
from jax.sharding import PartitionSpec as P

MESH = pl.DeviceIdType.MESH
F32 = jnp.float32
BF16 = jnp.bfloat16
HIGHEST = lax.Precision.HIGHEST

route_scale = 2.5
norm_eps = 1e-06

D = 3584
HID = 256
TOK = 128
ROWS = 256
HALF = D // 2
QUART = D // 4
PIECES = ((0, 0, 512), (0, 512, 384), (1, 0, 640), (1, 640, 256))
COUNT = len(PIECES)


def dot(a, b):
    return jnp.dot(a, b, preferred_element_type=F32)


def dot_nt(a, b, precision=None):
    return lax.dot_general(
        a, b, (((1,), (1,)), ((), ())), preferred_element_type=F32, precision=precision
    )


def iota(shape, dim):
    return lax.broadcasted_iota(jnp.int32, shape, dim)


def at128(start, size):
    return pl.ds(pl.multiple_of(start, 128), size)


def at16(start, size):
    return pl.ds(pl.multiple_of(start, 16), size)


def at8(start, size):
    return pl.ds(pl.multiple_of(start, 8), size)


def split(value):
    high = value.astype(BF16)
    return high, (value - high.astype(F32)).astype(BF16)


def kernel(
    tok_h,
    cot_h,
    gain_h,
    rout_h,
    wg_h,
    wu_h,
    wd_h,
    ids_h,
    out_v,
    grad_v,
    ids,
    gain,
    rout,
    hid,
    cot,
    nrm,
    wg,
    wu,
    wd,
    sel,
    com,
    cwh,
    cwl,
    inv_s,
    log_s,
    send,
    full,
    act_g,
    gv,
    uv,
    act,
    gg,
    ug,
    sc,
    scs,
    scr,
    lsem,
    d_s,
    d_r,
    f_s,
    f_r,
    s_s,
    s_r,
    e_s,
    e_r,
    p_s,
    p_r,
    r_s,
    r_r,
    a_s,
    a_r,
    c_s,
    c_r,
    x_s,
    x_r,
    *piece_refs,
):
    bufs = [piece_refs[i * 12 : (i + 1) * 12] for i in range(COUNT)]

    px = lax.axis_index("pipe")
    ex = lax.axis_index("expert")
    dx = lax.axis_index("dp")
    y = ex // 4
    zh = ex % 4
    zl = dx // 2
    c = dx % 2
    near = (zh + 2 * zl + 3) % 4
    far = (zh + 2) % 4
    opp = (zh + 5 - 2 * zl) % 4
    me = zh * 4 + y
    other = 1 - zl
    ys = [(y + dy) % 4 for dy in range(4)]
    yb = [(y + 4 - dy) % 4 for dy in range(4)]

    def dev(zh_, y_, zl_, c_):
        return (px, y_ * 4 + zh_, zl_ * 2 + c_)

    sibling = dev(zh, y, zl, 1 - c)
    partner = dev(zh, y, other, c)
    diagonal = dev(zh, y, other, 1 - c)
    after = ((px + 1) % 4, ex, dx)
    before = ((px + 3) % 4, ex, dx)

    def remote(src, dst, ssem, rsem, device):
        copy = pltpu.make_async_remote_copy(
            src_ref=src,
            dst_ref=dst,
            send_sem=ssem,
            recv_sem=rsem,
            device_id=device,
            device_id_type=MESH,
        )
        copy.start()
        return copy

    def take(ref, sem):
        pltpu.make_async_copy(ref, ref, sem).wait()

    barrier = pltpu.get_barrier_semaphore()
    greet = []
    for dy in (2, 1, 3, 0):
        greet += [
            dev(far, ys[dy], other, c),
            dev(near, ys[dy], zl, c),
            dev(opp, ys[dy], zl, c),
            dev(near, ys[dy], other, c),
        ]
        if dy:
            greet.append(dev(zh, ys[dy], zl, c))
    greet += [after, before, partner, diagonal, sibling]
    for device in greet:
        pl.semaphore_signal(barrier, inc=1, device_id=device, device_id_type=MESH)

    names = (ids, hid, gain, cot, wg, wu, wd, rout)
    sources = (ids_h, tok_h, gain_h, cot_h, wg_h, wu_h, wd_h, rout_h)
    loads = [
        pltpu.make_async_copy(a, b, lsem.at[i]) for i, (a, b) in enumerate(zip(sources, names))
    ]
    for load in loads[:3]:
        load.start()
    loads[0].wait()

    slot = iota((ROWS, TOK), 0)
    token = iota((ROWS, TOK), 1)
    slot_e = ((slot >> 4) & 3) * 4 + (slot >> 6)
    first = jnp.concatenate([ids[0, 0:1, :], ids[1, 0:1, :]], axis=1)
    second = jnp.concatenate([ids[0, 1:2, :], ids[1, 1:2, :]], axis=1)
    named = ((first == slot_e) | (second == slot_e)) & ((token >> 6) == ((slot >> 3) & 1))
    named = jnp.where(named, 1.0, 0.0)
    earlier = jnp.where(iota((TOK, TOK), 0) < iota((TOK, TOK), 1), 1.0, 0.0).astype(BF16)
    rank = dot(named.astype(BF16), earlier)
    picks = jnp.where(rank == (slot & 7).astype(F32), named, 0.0)
    sel[...] = picks.astype(BF16)

    half = c * HALF
    loads[1].wait()
    for load in loads[3:]:
        load.start()
    total = jnp.zeros((TOK, 1), F32)
    for i in range(4):
        part = hid[:, i * QUART : (i + 1) * QUART].astype(F32)
        total = total + jnp.sum(part * part, axis=1, keepdims=True)
    inv_s[...] = lax.rsqrt(total / D + norm_eps)

    def norm(start):
        for i in range(2):
            cols = at128(start + i * QUART, QUART)
            nrm[:, cols] = (hid[:, cols].astype(F32) * inv_s[...] * gain[:, cols]).astype(BF16)

    def gather(k, source):
        for i in range(2):
            send[k, :, i * QUART : (i + 1) * QUART] = dot(
                sel[...], source[:, at128(half + i * QUART, QUART)]
            ).astype(BF16)

    loads[2].wait()
    norm(half)
    gather(0, nrm)
    pl.semaphore_wait(barrier, len(greet))

    mine = at16(me * 16, 16)

    def send_near(k, dy):
        rows = at16((near * 4 + ys[dy]) * 16, 16)
        return remote(
            send.at[k, rows, :],
            full.at[k, mine, at128(half, HALF)],
            d_s.at[k],
            d_r.at[k, dy],
            dev(near, ys[dy], other, c),
        )

    def send_far(k, dy):
        rows = at16((far * 4 + ys[dy]) * 16, 16)
        return remote(
            send.at[k, rows, at128(zl * QUART, QUART)],
            full.at[k, mine, at128(half + zl * QUART, QUART)],
            d_s.at[k],
            d_r.at[k, 4 + dy],
            dev(far, ys[dy], other, c),
        )

    def send_own(k, dy):
        rows = at16((zh * 4 + ys[dy]) * 16, 16)
        return remote(
            send.at[k, rows, :],
            full.at[k, mine, at128(half, HALF)],
            d_s.at[k],
            d_r.at[k, 8],
            dev(zh, ys[dy], zl, c),
        )

    sent_x = [send_near(0, dy) for dy in range(4)]
    sent_x += [send_far(0, dy) for dy in range(4)]
    sent_x += [send_own(0, dy) for dy in range(1, 4)]
    full[0, mine, at128(half, HALF)] = send[0, mine, :]
    loads[3].wait()
    gather(1, cot)
    full[1, mine, at128(half, HALF)] = send[1, mine, :]

    def forward_near(k, sent):
        for dy in range(4):
            sent[dy].wait_recv()
            block = full.at[k, at16((near * 4 + yb[dy]) * 16, 16), at128(half, HALF)]
            remote(block, block, f_s.at[k], f_r.at[k, 0], partner)

    def forward_far(k, sent):
        for dy in range(4):
            sent[4 + dy].wait_recv()
            block = full.at[
                k,
                at16((far * 4 + yb[dy]) * 16, 16),
                at128(half + other * QUART, QUART),
            ]
            remote(block, block, f_s.at[k], f_r.at[k, 1], partner)

    def to_sibling(k, zh_):
        block = full.at[k, at16(zh_ * 64, 64), at128(half, HALF)]
        remote(block, block, s_s.at[k], s_r.at[k], sibling)

    def share_own(k):
        take(full.at[k, at16(zh * 64, 48), at128(half, HALF)], d_r.at[k, 8])
        to_sibling(k, zh)

    def share_opp(k):
        take(full.at[k, at16(opp * 64, 64), at128(half, HALF)], f_r.at[k, 0])
        to_sibling(k, opp)

    def share_far(k):
        take(full.at[k, at16(far * 64, 64), at128(half + zl * QUART, QUART)], f_r.at[k, 1])
        to_sibling(k, far)

    theirs = (1 - c) * HALF

    def complete(k):
        take(full.at[k, :, at128(theirs, HALF)], s_r.at[k])

    sent_u = [send_near(1, dy) for dy in range(4)]
    sent_u += [send_far(1, dy) for dy in range(4)]
    sent_u += [send_own(1, dy) for dy in range(1, 4)]
    forward_near(0, sent_x)
    to_sibling(0, near)
    forward_far(0, sent_x)
    share_own(0)

    com[...] = picks.T
    loads[7].wait()
    norm((1 - c) * HALF)
    log_s[...] = dot_nt(nrm[...], rout[...])
    spread = iota((16, ROWS), 1)
    spread = jnp.where(
        ((spread >> 4) & 3) * 4 + (spread >> 6) == iota((16, ROWS), 0), 1.0, 0.0
    )

    def chosen_parts():
        mask = dot_nt(com[...].astype(BF16), spread.astype(BF16))
        sig = jax.nn.sigmoid(log_s[...])
        csum = jnp.sum(mask * sig, axis=1, keepdims=True)
        return mask, sig, csum, route_scale * sig * mask / csum

    mask, sig, csum, w16 = chosen_parts()
    w_high, w_low = split(w16)
    cwh[...] = (dot(w_high, spread.astype(BF16)) * com[...]).astype(BF16)
    cwl[...] = (dot(w_low, spread.astype(BF16)) * com[...]).astype(BF16)

    share_opp(0)
    share_far(0)
    forward_near(1, sent_u)
    to_sibling(1, near)
    for load in loads[4:7]:
        load.wait()
    complete(0)

    gv[...] = dot(full[0], wg[...])
    uv[...] = dot(full[0], wu[...])
    g = gv[...]
    act[...] = (g * jax.nn.sigmoid(g) * uv[...]).astype(BF16)

    def down(cols):
        return dot(act[...], wd[:, cols])

    def back(cols):
        return dot_nt(gg[...], wg[cols, :]) + dot_nt(ug[...], wu[cols, :])

    terms = (down, back)
    def swap(p):
        k, off, w = PIECES[p]
        es, er = bufs[p][0], bufs[p][2]
        for i in range(2):
            es[:, i * w : (i + 1) * w] = terms[k](at128(theirs + i * QUART + off, w)).astype(BF16)
        return remote(es, er, e_s.at[p], e_r.at[p], sibling)

    def keep(p):
        k, off, w = PIECES[p]
        eo = bufs[p][1]
        for i in range(2):
            eo[:, i * w : (i + 1) * w] = terms[k](at128(half + i * QUART + off, w))

    def pair_sum(p, swapped):
        w = PIECES[p][2]
        es, eo, er, cp, pa, pb, pc = bufs[p][:7]
        swapped.wait_recv()

        def add(zh_):
            rows = at16(zh_ * 64, 64)
            cp[rows, :] = (eo[rows, :] + er[rows, :].astype(F32)).astype(BF16)
            return rows

        rows = add(far)
        copies = [
            remote(cp.at[rows, at128(zl * w, w)], pb, p_s.at[p], p_r.at[p, 0], partner)
        ]
        rows = add(opp)
        copies.append(remote(cp.at[rows, :], pa, p_s.at[p], p_r.at[p, 1], partner))
        rows = add(zh)
        copies.append(
            remote(cp.at[rows, at128(other * w, w)], pc, p_s.at[p], p_r.at[p, 2], partner)
        )
        add(near)
        return copies

    def give_back(p, pair):
        w = PIECES[p][2]
        cp, pa, pb, pc, fa, fb, fc, ret = bufs[p][3:11]

        def give(src, zh_, dy, zl_):
            remote(src, ret.at[mine, :], r_s.at[p], r_r.at[p], dev(zh_, ys[dy], zl_, c))

        pair[0].wait_recv()
        fb[...] = (
            cp[at16(far * 64, 64), at128(other * w, w)].astype(F32) + pb[...].astype(F32)
        ).astype(BF16)
        for dy in range(4):
            give(fb.at[at16(ys[dy] * 16, 16), :], far, dy, other)
        pair[1].wait_recv()
        fa[...] = (cp[at16(near * 64, 64), :].astype(F32) + pa[...].astype(F32)).astype(BF16)
        for dy in range(4):
            rows = at16(ys[dy] * 16, 16)
            give(fa.at[rows, at128(zl * w, w)], near, dy, zl)
            give(fa.at[rows, at128(other * w, w)], near, dy, other)
        pair[2].wait_recv()
        fc[...] = (
            cp[at16(zh * 64, 64), at128(zl * w, w)].astype(F32) + pc[...].astype(F32)
        ).astype(BF16)
        for dy in range(1, 4):
            give(fc.at[at16(ys[dy] * 16, 16), :], zh, dy, zl)
        ret[mine, :] = fc[at16(y * 16, 16), :]

    swaps = [swap(0), swap(1)]
    keep(0)
    forward_far(1, sent_u)
    share_own(1)
    pairs = [pair_sum(0, swaps[0])]
    share_opp(1)
    keep(1)
    pairs.append(pair_sum(1, swaps[1]))
    share_far(1)
    complete(1)

    act_g[...] = dot_nt(full[1], wd[...])
    g, u, a = gv[...], uv[...], act_g[...]
    sigma = jax.nn.sigmoid(g)
    gg[...] = (a * u * sigma * (1.0 + g * (1.0 - sigma))).astype(BF16)
    ug[...] = (a * g * sigma).astype(BF16)
    swaps += [swap(2), swap(3)]
    ones = jnp.ones((8, HID), F32)
    w_row = dot_nt(ones, act[...].astype(F32) * act_g[...], HIGHEST)
    n_row = dot_nt(
        ones, gg[...].astype(F32) * gv[...] + ug[...].astype(F32) * uv[...], HIGHEST
    )
    line = iota((8, ROWS), 0)
    sc[dx] = jnp.where(line == 0, w_row, jnp.where(line == 1, n_row, 0.0))
    for device in (sibling, partner, diagonal):
        remote(sc.at[dx], sc.at[dx], a_s.at[0], a_r.at[0], device)
    give_back(0, pairs[0])

    keep(2)
    pairs.append(pair_sum(2, swaps[2]))
    keep(3)
    give_back(1, pairs[1])
    pairs.append(pair_sum(3, swaps[3]))

    quarter = half + zl * QUART
    results = (out_v, grad_v)

    def combine(p):
        ret = bufs[p][10]
        take(ret.at[0:240, :], r_r.at[p])
        return dot(cwh[...], ret[...]) + dot(cwl[...], ret[...])

    def ship(p, value, device):
        k, off, w = PIECES[p]
        fin = bufs[p][11]
        fin[...] = value.astype(BF16)
        return remote(
            fin, results[k].at[:, at128(quarter + off, w)], x_s.at[p], x_r.at[p, 0], device
        )

    def pass_on(p, shift):
        k, off, w = PIECES[p]
        shift.wait_recv()
        block = results[k].at[:, at128(quarter + off, w)]
        remote(block, block, x_s.at[p], x_r.at[p, 2], sibling)
        return remote(block, block, x_s.at[p], x_r.at[p, 1], partner)

    def pass_last(p, passed):
        k, off, w = PIECES[p]
        passed.wait_recv()
        block = results[k].at[:, at128(half + other * QUART + off, w)]
        remote(block, block, x_s.at[p], x_r.at[p, 2], sibling)

    def forward_result(p):
        k, off, w = PIECES[p]
        return hid[:, at128(quarter + off, w)].astype(F32) + combine(p)

    shifts = [ship(0, forward_result(0), after)]
    shifts.append(ship(1, forward_result(1), after))
    take(sc.at[0:3], a_r.at[0])
    scs[...] = (sc[0] + sc[1]) + (sc[2] + sc[3])
    own_notes = at8(me * 8, 8)
    for dy in range(4):
        for zh_, zl_ in ((near, other), (near, zl), (far, other)) + (((zh, zl),) if dy else ()):
            remote(
                scs.at[:, at128((zh_ // 2) * 128, 128)],
                scr.at[own_notes, :],
                c_s.at[0],
                c_r.at[0],
                dev(zh_, ys[dy], zl_, c),
            )
    scr[own_notes, :] = scs[:, at128((zh // 2) * 128, 128)]

    passed = [pass_on(0, shifts[0])]
    give_back(2, pairs[2])
    passed.append(pass_on(1, shifts[1]))
    give_back(3, pairs[3])

    take(scr.at[0:120, :], c_r.at[0])
    lane_at = (me % 8) * 16
    row, col = iota((128, ROWS), 0), iota((128, ROWS), 1)
    turn = jnp.where(row == lane_at + (col & 15), 1.0, 0.0)
    moved = jnp.dot(scr[...], turn, precision=HIGHEST, preferred_element_type=F32)
    own_row = (row >> 3) == (col >> 4)
    w_row = jnp.sum(jnp.where(own_row & ((row & 7) == 0), moved, 0.0), axis=0, keepdims=True)
    n_row = jnp.sum(jnp.where(own_row & ((row & 7) == 1), moved, 0.0), axis=0, keepdims=True)
    mask, sig, csum, w16 = chosen_parts()
    weight_grad = dot_nt(com[...] * w_row, spread, HIGHEST)
    total = jnp.sum(weight_grad * w16, axis=1, keepdims=True)
    logit_grad = (route_scale * weight_grad - total) / csum * sig * (1.0 - sig) * mask
    weighted = cwh[...].astype(F32) + cwl[...].astype(F32)
    inner = jnp.sum(weighted * n_row, axis=1, keepdims=True) + jnp.sum(
        logit_grad * log_s[...], axis=1, keepdims=True
    )
    l_high, l_low = split(logit_grad)
    inverse = inv_s[...]
    pull = inverse * inverse * inner / D

    def gradient(p):
        k, off, w = PIECES[p]
        cols = at128(quarter + off, w)
        routers = rout[:, cols]
        normed_grad = combine(p) + (dot(l_high, routers) + dot(l_low, routers))
        return (
            cot[:, cols].astype(F32)
            + inverse * gain[:, cols] * normed_grad
            - hid[:, cols].astype(F32) * pull
        )

    shifts.append(ship(2, gradient(2), before))
    pass_last(0, passed[0])
    pass_last(1, passed[1])
    shifts.append(ship(3, gradient(3), before))
    passed.append(pass_on(2, shifts[2]))
    passed.append(pass_on(3, shifts[3]))
    pass_last(2, passed[2])
    pass_last(3, passed[3])
    for p in range(COUNT):
        take(bufs[p][10], x_r.at[p, 2])
    for k in range(2):
        take(send.at[k, 0:144, :], d_s.at[k])
        take(send.at[k, 0:96, :], f_s.at[k])
        take(send.at[k], s_s.at[k])
    for p in range(COUNT):
        es, cp, ret = bufs[p][0], bufs[p][3], bufs[p][10]
        take(es, e_s.at[p])
        take(cp.at[0:128, :], p_s.at[p])
        take(ret.at[0:240, :], r_s.at[p])
        take(es, x_s.at[p])
    take(sc.at[0:3], a_s.at[0])
    take(scr.at[0:120, :], c_s.at[0])


def shards(tokens, cotangent, gain, router, w_gate, w_up, w_down, expert_ids):
    anywhere = pl.BlockSpec(memory_space=pl.ANY)
    vmem = pl.BlockSpec(memory_space=pltpu.VMEM)

    def buf(*shape, dtype=BF16):
        return pltpu.VMEM(shape, dtype)

    def sems(*shape):
        return pltpu.SemaphoreType.DMA(shape)

    scratch = [
        buf(2, 2, TOK // 2, dtype=jnp.int32),
        buf(1, D, dtype=F32),
        buf(16, D),
        buf(TOK, D),
        buf(TOK, D),
        buf(TOK, D),
        buf(D, HID),
        buf(D, HID),
        buf(HID, D),
        buf(ROWS, TOK),
        buf(TOK, ROWS, dtype=F32),
        buf(TOK, ROWS),
        buf(TOK, ROWS),
        buf(TOK, 1, dtype=F32),
        buf(TOK, 16, dtype=F32),
        buf(2, ROWS, HALF),
        buf(2, ROWS, D),
        buf(ROWS, HID, dtype=F32),
        buf(ROWS, HID, dtype=F32),
        buf(ROWS, HID, dtype=F32),
        buf(ROWS, HID),
        buf(ROWS, HID),
        buf(ROWS, HID),
        buf(4, 8, ROWS, dtype=F32),
        buf(8, ROWS, dtype=F32),
        buf(128, 128, dtype=F32),
        sems(8),
        sems(2),
        sems(2, 9),
        sems(2),
        sems(2, 2),
        sems(2),
        sems(2),
        sems(COUNT),
        sems(COUNT),
        sems(COUNT),
        sems(COUNT, 3),
        sems(COUNT),
        sems(COUNT),
        sems(1),
        sems(1),
        sems(1),
        sems(1),
        sems(COUNT),
        sems(COUNT, 3),
    ]
    for _, _, w in PIECES:
        scratch += [
            buf(ROWS, 2 * w),
            buf(ROWS, 2 * w, dtype=F32),
            buf(ROWS, 2 * w),
            buf(ROWS, 2 * w),
            buf(64, 2 * w),
            buf(64, w),
            buf(64, w),
            buf(64, 2 * w),
            buf(64, w),
            buf(64, w),
            buf(ROWS, w),
            buf(TOK, w),
        ]
    out = pltpu.VMEM((TOK, D), BF16)
    section_out, section_grad = pl.pallas_call(
        kernel,
        out_shape=(out, out),
        in_specs=[anywhere] * 8,
        out_specs=(vmem, vmem),
        scratch_shapes=scratch,
        compiler_params=pltpu.CompilerParams(
            collective_id=0, has_side_effects=True, vmem_limit_bytes=56 * 1024 * 1024
        ),
    )(
        tokens.reshape(TOK, D),
        cotangent.reshape(TOK, D),
        gain,
        jnp.swapaxes(router.reshape(D, 16), 0, 1),
        w_gate.reshape(D, HID),
        w_up.reshape(D, HID),
        w_down.reshape(HID, D),
        jnp.swapaxes(expert_ids.reshape(2, TOK // 2, 2), 1, 2),
    )
    return section_out.reshape(tokens.shape), section_grad.reshape(tokens.shape)


def solution(mesh):
    in_specs = (
        P("pipe", None, "expert", None),
        P("pipe", None, "expert", None),
        P("pipe", None),
        P("pipe", None, None),
        P("pipe", "expert", None, "dp"),
        P("pipe", "expert", None, "dp"),
        P("pipe", "expert", "dp", None),
        P("pipe", None, "expert", None),
    )
    out_specs = (P("pipe", None, "expert", None), P("pipe", None, "expert", None))
    return jax.shard_map(shards, mesh=mesh, in_specs=in_specs, out_specs=out_specs, check_vma=False)
```
